32 devices in a mesh: line: 8 (over y, x, core), bus: 4 (over z).
Axes of the slice: x: 2, y: 2, z: 4, core: 2. Of those that a mesh axis runs over, the one named last changes fastest.
Arguments:
- ptdf: bfloat16 [2048, 100352], P('line', 'bus')
- base_injection: float32 [100352], P('bus'), may hold values from -6 to 6
- injection_gain: float32 [100352], P('bus'), may hold values from 0.3 to 3
- factor_of_bus: int32 [100352], P('bus'), may hold values from 0 to 511
- line_rating: int32 [2048], P('line'), may hold values from 60 to 300
- directions: int32 [30, 512], replicated, may hold values from 1 to 1073741823, as said below
- shifts: int32 [8, 512], replicated, may hold values from 0 to 1073741823
- chol_factor: float32 [512, 512], replicated
- proposal_mean: float32 [512], replicated, may hold values from -0.3 to 0.3
Outputs:
- flows: float32 [1024, 2048], P('bus', 'line')
- overload: float32 [1024], P('bus')
- weight: float32 [1024], P('bus')
- new_mean: float32 [512], replicated
The draws below stay inside these ranges and needn't reach their ends.
Inputs may be any that keep to these rules, and one draw needn't show every extreme that they name: directions[b, f] lies in [2^(29 - b), 2^(30 - b)), as Sobol direction numbers do.
All inputs are finite; a program needn't handle non-finite values.
Results may differ from the reference program's by a relative error of at most 0.0029.
Values sent between devices are 32-bit elements; how exact they have to be, the bound alone decides.
No kernel may reach another device: no remote copies, remote signals or barrier semaphores. Data moves between devices by JAX's collectives and lax.ppermute only.
A program may use at most 64 MiB of HBM per device.

```python
import math
import jax
import jax.numpy as jnp
from jax import lax

BUS = 100352
FACTORS = 512
BITS = 30
SHIFTS = 8
POINTS = 128
SCEN = 1024
LINES = 2048


def draw_directions(key, part):
    bit_rows = jnp.arange(BITS, dtype=jnp.int32)[:, None]
    leading = jnp.left_shift(jnp.ones((BITS, FACTORS), jnp.int32), 29 - bit_rows)
    noise = jax.random.randint(key, (BITS, FACTORS), 0, 1073741824, dtype=jnp.int32)
    return leading + jnp.bitwise_and(noise, leading - 1)


def draw_chol_factor(key, part):
    entry_key = jax.random.fold_in(key, 11)
    diag_key = jax.random.fold_in(key, 12)
    entries = jax.random.normal(entry_key, (FACTORS, FACTORS), jnp.float32)
    diagonal = jnp.exp(jax.random.uniform(diag_key, (FACTORS,), jnp.float32, math.log(0.5), math.log(1.5)))
    lower = jnp.tril(entries, -1) * (0.8 / math.sqrt(FACTORS))
    return lower + jnp.eye(FACTORS, dtype=jnp.float32) * diagonal[None, :]


def draw_ptdf(key, part):
    entry_key = jax.random.fold_in(key, 21)
    row_key = jax.random.fold_in(key, 22)
    column_key = jax.random.fold_in(key, 23)
    position = jnp.arange(LINES, dtype=jnp.float32) / LINES
    entries = jax.random.normal(entry_key, (LINES, BUS), jnp.float32)
    row_spread = jnp.exp(jax.random.uniform(row_key, (LINES,), jnp.float32, math.log(0.5), math.log(2.0)))
    column_spread = jnp.exp(jax.random.uniform(column_key, (BUS,), jnp.float32, math.log(0.5), math.log(2.0)))
    row_scale = jnp.exp(math.log(3.0) * position) * row_spread
    values = entries * row_scale[:, None] * column_spread[None, :] * (0.5 / math.sqrt(BUS))
    return values.astype(jnp.bfloat16)


def set_ends(values, key, low, largest):
    longest = values.shape.index(max(values.shape))
    spots = []
    for shift in (0, 1):
        where = [jax.random.randint(jax.random.fold_in(key, axis), (), 0, length) for axis, length in enumerate(values.shape)]
        where[longest] = (where[longest] + shift) % values.shape[longest]
        spots.append(tuple(where))
    return values.at[spots[0]].set(low).at[spots[1]].set(largest)


def block_scale(rng, shape, cuts, low, top_value):
    level, own = 1.0, jax.random.fold_in(rng, 6)
    for dim, blocks in cuts:
        steps = jnp.exp(jax.random.uniform(jax.random.fold_in(own, dim), (blocks,), jnp.float32, low / len(cuts), top_value / len(cuts)))
        level = level * jnp.repeat(steps, shape[dim] // blocks).reshape([-1 if axis == dim else 1 for axis in range(len(shape))])
    return level


def bell_draw(rng, dims, scale, reach, split=(), kind=jnp.bfloat16):
    drawn = jax.random.normal(rng, dims, jnp.float32) * scale
    if len(split) > 0:
        drawn = block_scale(rng, dims, split, -0.22, 0.18) * drawn
    return jnp.clip(drawn, min=-reach, max=reach).astype(kind)


def setup_inputs(seed: int = 0) -> dict:
    arg_keys = jax.random.split(jax.random.key(seed), 10)
    return {
        "ptdf": draw_ptdf(jax.random.fold_in(arg_keys[9], 71), 0),
        "base_injection": bell_draw(arg_keys[1], (BUS,), 1.0, 6.0, ((0, 4),), jnp.float32),
        "injection_gain": jnp.clip(jnp.exp(math.log(3.0) - 2.3025851 * jax.random.uniform(arg_keys[2], (BUS,), jnp.float32) ** block_scale(arg_keys[2], (BUS,), ((0, 4),), -0.2, 0.2)), 0.3, 3.0),
        "factor_of_bus": set_ends(jax.random.randint(arg_keys[3], (BUS,), 0, FACTORS), jax.random.fold_in(arg_keys[3], 1), 0, FACTORS - 1).astype(jnp.int32),
        "line_rating": set_ends(jax.random.randint(arg_keys[4], (LINES,), 60, 301), jax.random.fold_in(arg_keys[4], 1), 60, 300).astype(jnp.int32),
        "directions": draw_directions(jax.random.fold_in(arg_keys[9], 71), 0),
        "shifts": set_ends(jax.random.randint(arg_keys[6], (SHIFTS, FACTORS), 0, 1073741824), jax.random.fold_in(arg_keys[6], 1), 0, 1073741823).astype(jnp.int32),
        "chol_factor": draw_chol_factor(jax.random.fold_in(arg_keys[9], 71), 0),
        "proposal_mean": bell_draw(arg_keys[8], (FACTORS,), 0.06, 0.3, (), jnp.float32),
    }


SHARP = 8.0

def normals(directions, shifts, start_row, row_count):
    scenario = start_row + jnp.arange(row_count, dtype=jnp.int32)
    sobol_point = scenario % POINTS
    shift_index = scenario // POINTS
    digits = jnp.zeros((row_count, directions.shape[1]), jnp.int32)
    for bit_index in range(max(1, (POINTS - 1).bit_length())):
        picked = sobol_point >> bit_index & 1
        digits = digits ^ picked[:, None] * directions[bit_index][None, :]
    chosen = (shift_index[:, None] == jnp.arange(shifts.shape[0], dtype=jnp.int32)[None, :]).astype(jnp.int32)
    offset = lax.optimization_barrier(jnp.sum(chosen[:, :, None] * shifts[None, :, :], axis=1))
    digits = digits ^ offset
    uniform = (2 * (digits >> 7) + 1).astype(jnp.float32) / 16777216.0
    return math.sqrt(2.0) * lax.erf_inv(2.0 * uniform - 1.0)

def reference(ptdf, base_injection, injection_gain, factor_of_bus, line_rating, directions, shifts, chol_factor, proposal_mean):
    high = lax.Precision.HIGHEST
    normal_draws = normals(directions, shifts, 0, SCEN)
    factors = jnp.dot(normal_draws + proposal_mean[None, :], chol_factor.T, precision=high, preferred_element_type=jnp.float32)
    picked = jnp.take(factors, factor_of_bus, axis=1)
    injections = (base_injection[None, :] + injection_gain[None, :] * picked).astype(jnp.bfloat16)
    wide_injections = injections.astype(jnp.float32)
    line_block = 512 if LINES % 512 == 0 else LINES
    blocks = ptdf.reshape(LINES // line_block, line_block, ptdf.shape[1])

    def one_block(rows):
        return jnp.dot(wide_injections, rows.astype(jnp.float32).T, precision=high, preferred_element_type=jnp.float32)
    flows = lax.map(one_block, blocks)
    flows = jnp.transpose(flows, (1, 0, 2)).reshape(SCEN, LINES)
    rating = line_rating.astype(jnp.float32) * 0.01
    overload = lax.optimization_barrier(jnp.sum(jax.nn.softplus(SHARP * (jnp.abs(flows) / rating[None, :] - 1.0)), axis=1)) / SHARP / LINES
    likelihood = jnp.exp(-jnp.dot(normal_draws, proposal_mean, precision=high, preferred_element_type=jnp.float32))
    emphasis = likelihood * overload
    total = jnp.sum(emphasis)
    weight = SCEN * likelihood * overload / total
    new_mean = proposal_mean + jnp.dot(emphasis, normal_draws, precision=high, preferred_element_type=jnp.float32) / total
    return (flows, overload, weight, new_mean)
```

```python
import math

import jax
import jax.numpy as jnp
from jax import lax
from jax.experimental import pallas as pl
from jax.experimental.pallas import tpu as pltpu
from jax.sharding import PartitionSpec as P

POINTS = 128
SHARP = 8.0
HIGH = lax.Precision.HIGHEST
NT = (((1,), (1,)), ((), ()))
LANES = 128
EXTRA = 16


def normals(directions, shifts, start_row, row_count):
    scenario = start_row + jnp.arange(row_count, dtype=jnp.int32)
    sobol_point = scenario % POINTS
    shift_index = scenario // POINTS
    digits = jnp.zeros((row_count, directions.shape[1]), jnp.int32)
    for bit_index in range(max(1, (POINTS - 1).bit_length())):
        picked = sobol_point >> bit_index & 1
        digits = digits ^ picked[:, None] * directions[bit_index][None, :]
    chosen = (shift_index[:, None] == jnp.arange(shifts.shape[0], dtype=jnp.int32)[None, :]).astype(
        jnp.int32
    )
    offset = jnp.sum(chosen[:, :, None] * shifts[None, :, :], axis=1)
    digits = digits ^ offset
    uniform = (2 * (digits >> 7) + 1).astype(jnp.float32) / 16777216.0
    return math.sqrt(2.0) * lax.erf_inv(2.0 * uniform - 1.0)


def block_width(buses):
    for width in (3584, 1792, 896, 512, 256):
        if buses % width == 0:
            return width
    return LANES


def segment_sums(ptdf, base, gain, factor, n_factors):
    lines, buses = ptdf.shape
    width = block_width(buses)
    blocks, rows, per = buses // width, buses // LANES, width // LANES

    def body(p_hbm, b_hbm, g_hbm, f_hbm, out, p_v, b_v, g_v, f_v, p_sem, v_sem):
        vectors = [
            pltpu.make_async_copy(h, v, v_sem.at[i])
            for i, (h, v) in enumerate(((f_hbm, f_v), (g_hbm, g_v), (b_hbm, b_v)))
        ]
        for copy in vectors:
            copy.start()

        def block_copy(k):
            at = pl.ds(pl.multiple_of(k * width, width), width)
            return pltpu.make_async_copy(p_hbm.at[:, at], p_v.at[:, at], p_sem.at[k])

        def start(k, _):
            block_copy(k).start()
            return 0

        lax.fori_loop(0, blocks, start, 0)
        out[...] = jnp.zeros_like(out)
        for copy in vectors:
            copy.wait()

        def step(k, _):
            block_copy(k).wait()

            def row(v):
                return jnp.concatenate([v[pl.ds(k * per + j, 1), :] for j in range(per)], 1)

            g = row(g_v)
            p = p_v[:, pl.ds(pl.multiple_of(k * width, width), width)]
            scaled = (p.astype(jnp.float32) * g).astype(jnp.bfloat16)
            own = lax.broadcasted_iota(jnp.int16, (n_factors, width), 0) == row(f_v).astype(jnp.int16)
            hot = jnp.where(own, jnp.bfloat16(1), jnp.bfloat16(0))
            ratio = row(b_v) / g
            high = ratio.astype(jnp.bfloat16)
            low = (ratio - high.astype(jnp.float32)).astype(jnp.bfloat16)
            rest = jnp.zeros((EXTRA - 2, width), jnp.bfloat16)
            left = jnp.concatenate([hot, high, low, rest], 0)
            out[...] += lax.dot_general(left, scaled, NT, preferred_element_type=jnp.float32)
            return 0

        lax.fori_loop(0, blocks, step, 0)

    hbm = pl.BlockSpec(memory_space=pl.ANY)
    return pl.pallas_call(
        body,
        in_specs=[hbm] * 4,
        out_specs=pl.BlockSpec(memory_space=pltpu.VMEM),
        out_shape=jax.ShapeDtypeStruct((n_factors + EXTRA, lines), jnp.float32),
        scratch_shapes=[
            pltpu.VMEM((lines, buses), jnp.bfloat16),
            pltpu.VMEM((rows, LANES), jnp.float32),
            pltpu.VMEM((rows, LANES), jnp.float32),
            pltpu.VMEM((rows, LANES), jnp.int32),
            pltpu.SemaphoreType.DMA((blocks,)),
            pltpu.SemaphoreType.DMA((3,)),
        ],
        compiler_params=pltpu.CompilerParams(vmem_limit_bytes=48 * 2**20),
        cost_estimate=pl.CostEstimate(
            flops=2 * lines * buses * n_factors, bytes_accessed=2 * lines * buses, transcendentals=0
        ),
        name="segment_sums",
    )(ptdf, base.reshape(rows, LANES), gain.reshape(rows, LANES), factor.reshape(rows, LANES))


def xor_sum(value, axis):
    size = lax.axis_size(axis)
    if size & (size - 1):
        return lax.psum(value, axis)
    bit = 1
    while bit < size:
        value = value + lax.ppermute(value, axis, [(i, i ^ bit) for i in range(size)])
        bit *= 2
    return value


def per_device(
    ptdf,
    base_injection,
    injection_gain,
    factor_of_bus,
    line_rating,
    directions,
    shifts,
    chol_factor,
    proposal_mean,
):
    bus_devices = lax.axis_size("bus")
    lines_total = ptdf.shape[0] * lax.axis_size("line")
    n_factors = directions.shape[1]
    scenarios = POINTS * shifts.shape[0]
    block_rows = scenarios // bus_devices
    z = lax.axis_index("bus")

    sums = segment_sums(ptdf, base_injection, injection_gain, factor_of_bus, n_factors)
    per_factor, base_flow = sums[:n_factors], sums[n_factors] + sums[n_factors + 1]

    def draws(block, count=block_rows):
        return normals(directions, shifts, block * block_rows, count)

    def part(normal):
        factors = lax.dot_general(
            normal + proposal_mean[None, :],
            chol_factor,
            NT,
            precision=lax.Precision.HIGH,
            preferred_element_type=jnp.float32,
        )
        return base_flow[None, :] + jnp.dot(
            factors, per_factor, precision=lax.Precision.HIGH, preferred_element_type=jnp.float32
        )

    own_normals = draws(z)
    if bus_devices == 4:
        near = [(0, 1), (1, 0), (2, 3), (3, 2)]
        across = [(0, 3), (3, 0), (1, 2), (2, 1)]
        pair = part(draws(z ^ 3)) + lax.ppermute(part(draws(z ^ 2)), "bus", near)
        far = lax.ppermute(pair, "bus", across)
        beside = lax.ppermute(part(draws(z ^ 1)), "bus", near)
        flows = part(own_normals) + far + beside
    else:
        flows = lax.psum_scatter(part(draws(0, scenarios)), "bus", scatter_dimension=0, tiled=True)

    rating = line_rating.astype(jnp.float32) * 0.01
    likelihood = jnp.exp(
        -jnp.dot(own_normals, proposal_mean, precision=HIGH, preferred_element_type=jnp.float32)
    )
    share = jnp.sum(jax.nn.softplus(SHARP * (jnp.abs(flows) / rating[None, :] - 1.0)), axis=1)
    overload = xor_sum(share, "line") / SHARP / lines_total
    emphasis = likelihood * overload
    moved_part = jnp.dot(emphasis, own_normals, precision=HIGH, preferred_element_type=jnp.float32)
    sent = jnp.concatenate([moved_part, jnp.full((LANES,), jnp.sum(emphasis))])
    got = xor_sum(sent, "bus")
    moved, total = got[:n_factors], got[n_factors]
    weight = scenarios * likelihood * overload / total
    new_mean = proposal_mean + moved / total
    return (flows, overload, weight, new_mean)


def solution(mesh):
    return jax.shard_map(
        per_device,
        mesh=mesh,
        in_specs=(P("line", "bus"), P("bus"), P("bus"), P("bus"), P("line"), P(), P(), P(), P()),
        out_specs=(P("bus", "line"), P("bus"), P("bus"), P()),
        check_vma=False,
    )
```

```python
import math

import jax
import jax.numpy as jnp
from jax import lax
from jax.experimental import pallas as pl
from jax.experimental.pallas import tpu as pltpu
from jax.sharding import PartitionSpec as P

POINTS = 128
SHARP = 8.0
HIGH = lax.Precision.HIGH
HIGHEST = lax.Precision.HIGHEST
NT = (((1,), (1,)), ((), ()))
NN = (((1,), (0,)), ((), ()))
LANES = 128
EXTRA = 16
MIB = 2**20
CENTRAL = (
    2.81022636e-08, 3.43273939e-07, -3.5233877e-06, -4.39150654e-06, 0.00021858087,
    -0.00125372503, -0.00417768164, 0.246640727, 1.50140941,
)
TAIL = (
    -0.000200214257, 0.000100950558, 0.00134934322, -0.00367342844, 0.00573950773,
    -0.0076224613, 0.00943887047, 1.00167406, 2.83297682,
)


def dot(a, b, dims, precision):
    return lax.dot_general(a, b, dims, precision=precision, preferred_element_type=jnp.float32)


def normal_of(digits):
    x = (2 * (digits >> 7) + 1).astype(jnp.float32) * (2.0 / 16777216.0) - 1.0
    w = -jnp.log((1.0 - x) * (1.0 + x))
    central = w < 5.0
    w = jnp.where(central, w - 2.5, jnp.sqrt(w) - 3.0)
    p = jnp.where(central, CENTRAL[0], TAIL[0])
    for a, b in zip(CENTRAL[1:], TAIL[1:]):
        p = jnp.where(central, a, b) + p * w
    return math.sqrt(2.0) * (p * x)


def block_normals(directions, shifts, start, rows):
    group = min(rows, POINTS)
    n = directions.shape[1]
    digits = jnp.zeros((1, n), jnp.int32)
    bits = group.bit_length() - 1
    lead = min(bits, 3)
    at = lax.broadcasted_iota(jnp.int32, (2**lead, n), 0)
    digits = jnp.zeros((2**lead, n), jnp.int32)
    for b in range(lead):
        digits = digits ^ jnp.where((at >> b & 1) == 1, directions[b : b + 1, :], 0)
    for b in range(lead, bits):
        digits = jnp.concatenate([digits, digits ^ directions[b : b + 1, :]], 0)
    pieces = []
    for j in range(rows // group):
        first = start + j * group
        point = lax.rem(first, POINTS)
        flip = shifts[pl.ds(lax.div(first, POINTS), 1), :]
        for b in range(bits, POINTS.bit_length() - 1):
            flip = flip ^ (directions[b : b + 1, :] * (point >> b & 1))
        pieces.append(normal_of(digits ^ flip))
    return jnp.concatenate(pieces, 0) if len(pieces) > 1 else pieces[0]


def block_width(buses):
    for width in (3584, 1792, 896, 512, 256):
        if buses % width == 0:
            return width
    return LANES


def head(blocks, ptdf, base, gain, factor, directions, shifts, chol, mean, block_rows):
    lines, buses = ptdf.shape
    n = directions.shape[1]
    width = block_width(buses)
    steps, rows, per = buses // width, buses // LANES, width // LANES

    def body(
        blocks_s, p_h, b_h, g_h, f_h, d_h, s_h, c_h, m_h,
        sums, part, p_v, b_v, g_v, f_v, d_v, s_v, c_v, m_v, p_sem, v_sem,
    ):
        pairs = ((d_h, d_v), (s_h, s_v), (c_h, c_v), (m_h, m_v), (f_h, f_v), (g_h, g_v), (b_h, b_v))
        small = [pltpu.make_async_copy(h, v, v_sem.at[i]) for i, (h, v) in enumerate(pairs)]
        for copy in small:
            copy.start()

        def block_copy(k):
            at = pl.ds(pl.multiple_of(k * width, width), width)
            return pltpu.make_async_copy(p_h.at[:, at], p_v.at[:, at], p_sem.at[k])

        def start(k, _):
            block_copy(k).start()
            return 0

        lax.fori_loop(0, steps, start, 0)
        sums[...] = jnp.zeros_like(sums)
        for copy in small:
            copy.wait()
        draws = block_normals(d_v, s_v, blocks_s[0] * block_rows, block_rows)
        factors = dot(draws + m_v[...], c_v[...], NT, HIGH)

        def step(k, _):
            block_copy(k).wait()

            def row(v):
                return jnp.concatenate([v[pl.ds(k * per + j, 1), :] for j in range(per)], 1)

            g = row(g_v)
            p = p_v[:, pl.ds(pl.multiple_of(k * width, width), width)]
            scaled = (p.astype(jnp.float32) * g).astype(jnp.bfloat16)
            own = lax.broadcasted_iota(jnp.int16, (n, width), 0) == row(f_v).astype(jnp.int16)
            hot = jnp.where(own, jnp.bfloat16(1), jnp.bfloat16(0))
            ratio = row(b_v) / g
            high = ratio.astype(jnp.bfloat16)
            low = (ratio - high.astype(jnp.float32)).astype(jnp.bfloat16)
            rest = jnp.zeros((EXTRA - 2, width), jnp.bfloat16)
            left = jnp.concatenate([hot, high, low, rest], 0)
            sums[...] += lax.dot_general(left, scaled, NT, preferred_element_type=jnp.float32)
            return 0

        lax.fori_loop(0, steps, step, 0)
        base_row = sums[n : n + 1, :] + sums[n + 1 : n + 2, :]
        part[...] = dot(factors, sums[:n, :], NN, HIGH) + base_row

    hbm = pl.BlockSpec(memory_space=pltpu.HBM)
    vmem = pl.BlockSpec(memory_space=pltpu.VMEM)
    return pl.pallas_call(
        body,
        in_specs=[pl.BlockSpec(memory_space=pltpu.SMEM)] + [hbm] * 8,
        out_specs=[vmem, vmem],
        out_shape=[
            jax.ShapeDtypeStruct((n + EXTRA, lines), jnp.float32),
            jax.ShapeDtypeStruct((block_rows, lines), jnp.float32),
        ],
        scratch_shapes=[
            pltpu.VMEM((lines, buses), jnp.bfloat16),
            pltpu.VMEM((rows, LANES), jnp.float32),
            pltpu.VMEM((rows, LANES), jnp.float32),
            pltpu.VMEM((rows, LANES), jnp.int32),
            pltpu.VMEM(directions.shape, jnp.int32),
            pltpu.VMEM(shifts.shape, jnp.int32),
            pltpu.VMEM(chol.shape, jnp.float32),
            pltpu.VMEM((1, n), jnp.float32),
            pltpu.SemaphoreType.DMA((steps,)),
            pltpu.SemaphoreType.DMA((7,)),
        ],
        compiler_params=pltpu.CompilerParams(vmem_limit_bytes=48 * MIB),
        cost_estimate=pl.CostEstimate(
            flops=2 * lines * buses * n, bytes_accessed=2 * lines * buses, transcendentals=0
        ),
        name="segment_sums",
    )(
        blocks,
        *(
            pltpu.with_memory_space_constraint(x, pltpu.HBM)
            for x in (
                ptdf, base.reshape(rows, LANES), gain.reshape(rows, LANES), factor.reshape(rows, LANES),
                directions, shifts, chol, mean.reshape(1, n),
            )
        ),
    )


def other_parts(blocks, sums, directions, shifts, chol, mean, block_rows):
    n = directions.shape[1]
    lines = sums.shape[1]

    def body(blocks_s, sums_v, d_v, s_v, c_v, m_v, part_1, part_2, part_3, draws, likelihood):
        base_row = sums_v[n : n + 1, :] + sums_v[n + 1 : n + 2, :]
        for i, part in enumerate((part_1, part_2, part_3)):
            draws[...] = block_normals(d_v, s_v, blocks_s[i + 1] * block_rows, block_rows)
            factors = dot(draws[...] + m_v[...], c_v[...], NT, HIGH)
            part[...] = dot(factors, sums_v[:n, :], NN, HIGH) + base_row
        tilt = dot(jnp.broadcast_to(m_v[...], (8, n)), draws[...], NT, HIGHEST)
        likelihood[...] = jnp.exp(-tilt)

    vmem = pl.BlockSpec(memory_space=pltpu.VMEM)
    shapes = [(block_rows, lines)] * 3 + [(block_rows, n), (8, block_rows)]
    return pl.pallas_call(
        body,
        in_specs=[pl.BlockSpec(memory_space=pltpu.SMEM)] + [vmem] * 5,
        out_specs=[vmem] * 5,
        out_shape=[jax.ShapeDtypeStruct(s, jnp.float32) for s in shapes],
        compiler_params=pltpu.CompilerParams(vmem_limit_bytes=32 * MIB),
        cost_estimate=pl.CostEstimate(
            flops=18 * block_rows * n * (n + lines), bytes_accessed=4 * MIB, transcendentals=6 * block_rows * n
        ),
        name="other_parts",
    )(blocks, sums, directions, shifts, chol, mean.reshape(1, n))


def finish_flows(mine, far, beside, rating, draws, likelihood, lines_total):
    rows, lines = mine.shape
    n = draws.shape[1]
    packed_rows = -(-(rows // LANES + n // LANES + 1) // 8) * 8

    def body(mine_v, far_v, beside_v, rating_v, draws_v, like_v, flows, packed):
        value = mine_v[...] + far_v[...] + beside_v[...]
        flows[...] = value
        limit = jnp.concatenate([rating_v[j : j + 1, :] for j in range(lines // LANES)], 1)
        limit = limit.astype(jnp.float32) * 0.01
        over = SHARP * (jnp.abs(value) / limit - 1.0)
        soft = jnp.maximum(over, 0.0) + jnp.log1p(jnp.exp(-jnp.abs(over)))
        share = dot(jnp.ones((8, lines), jnp.float32), soft, NT, HIGHEST) * (1.0 / SHARP / lines_total)
        emphasis = like_v[...] * share
        moved = dot(emphasis, draws_v[...], NN, HIGHEST)
        total = jnp.sum(emphasis[:1, :], axis=1, keepdims=True)
        parts = [share[:1, j * LANES : (j + 1) * LANES] for j in range(rows // LANES)]
        parts += [moved[:1, j * LANES : (j + 1) * LANES] for j in range(n // LANES)]
        parts += [jnp.broadcast_to(total, (1, LANES))]
        parts += [jnp.zeros((1, LANES), jnp.float32)] * (packed_rows - len(parts))
        packed[...] = jnp.concatenate(parts, 0)

    vmem = pl.BlockSpec(memory_space=pltpu.VMEM)
    return pl.pallas_call(
        body,
        in_specs=[vmem] * 6,
        out_specs=[vmem] * 2,
        out_shape=[
            jax.ShapeDtypeStruct((rows, lines), jnp.float32),
            jax.ShapeDtypeStruct((packed_rows, LANES), jnp.float32),
        ],
        compiler_params=pltpu.CompilerParams(vmem_limit_bytes=32 * MIB),
        name="finish_flows",
    )(mine, far, beside, rating.reshape(lines // LANES, LANES), draws, likelihood)


def last_outputs(own, others, likelihood, mean, scenarios):
    rows, n = likelihood.shape[1], mean.shape[0]
    a, b = rows // LANES, n // LANES

    def body(own_v, *refs):
        others_v, (like_v, mean_v, overload, weight, new_mean) = refs[:-5], refs[-5:]
        mine = own_v[...]
        everyone = mine
        for other in others_v:
            everyone = everyone + other[...]
        total = everyone[a + b : a + b + 1, :]
        like = jnp.concatenate([like_v[:1, j * LANES : (j + 1) * LANES] for j in range(a)], 0)
        overload[...] = mine[:a, :]
        weight[...] = scenarios * like * mine[:a, :] / total
        new_mean[...] = mean_v[...] + everyone[a : a + b, :] / total

    vmem = pl.BlockSpec(memory_space=pltpu.VMEM)
    shapes = [(a, LANES), (a, LANES), (b, LANES)]
    out = pl.pallas_call(
        body,
        in_specs=[vmem] * (3 + len(others)),
        out_specs=[vmem] * 3,
        out_shape=[jax.ShapeDtypeStruct(s, jnp.float32) for s in shapes],
        name="last_outputs",
    )(own, *others, likelihood, mean.reshape(b, LANES))
    return [x.reshape(-1) for x in out]


def xor_sum(value, axis):
    size = lax.axis_size(axis)
    if size & (size - 1):
        return lax.psum(value, axis)
    bit = 1
    while bit < size:
        value = value + lax.ppermute(value, axis, [(i, i ^ bit) for i in range(size)])
        bit *= 2
    return value


def normals(directions, shifts):
    point = jnp.arange(POINTS, dtype=jnp.int32)
    digits = jnp.zeros((POINTS, directions.shape[1]), jnp.int32)
    for b in range(POINTS.bit_length() - 1):
        digits = digits ^ (point >> b & 1)[:, None] * directions[b][None, :]
    return normal_of(digits[None, :, :] ^ shifts[:, None, :]).reshape(-1, directions.shape[1])


def per_device(
    ptdf,
    base_injection,
    injection_gain,
    factor_of_bus,
    line_rating,
    directions,
    shifts,
    chol_factor,
    proposal_mean,
):
    bus_devices = lax.axis_size("bus")
    lines_total = ptdf.shape[0] * lax.axis_size("line")
    n = directions.shape[1]
    scenarios = POINTS * shifts.shape[0]
    block_rows = scenarios // bus_devices
    z = lax.axis_index("bus").astype(jnp.int32)
    blocks = jnp.stack([z ^ 2, z ^ 3, z ^ 1, z]) if bus_devices == 4 else jnp.stack([z] * 4)
    drawn = (directions, shifts, chol_factor, proposal_mean)
    sums, first = head(
        blocks, ptdf, base_injection, injection_gain, factor_of_bus, *drawn, block_rows
    )

    if bus_devices == 4:
        near = [(0, 1), (1, 0), (2, 3), (3, 2)]
        across = [(0, 3), (3, 0), (1, 2), (2, 1)]
        from_near = lax.ppermute(first, "bus", near)
        second, third, mine, own_normals, likelihood = other_parts(blocks, sums, *drawn, block_rows)
        far = lax.ppermute(second + from_near, "bus", across)
        beside = lax.ppermute(third, "bus", near)
        flows, packed = finish_flows(
            mine, far, beside, line_rating, own_normals, likelihood, lines_total
        )
        packed = xor_sum(packed, "line")
        others = [
            lax.ppermute(packed, "bus", [(i, i ^ k) for i in range(bus_devices)])
            for k in range(1, bus_devices)
        ]
        overload, weight, new_mean = last_outputs(
            packed, others, likelihood, proposal_mean, scenarios
        )
        return (flows, overload, weight, new_mean)

    draws = normals(directions, shifts)
    factors = dot(draws + proposal_mean[None, :], chol_factor, NT, HIGH)
    part = dot(factors, sums[:n], NN, HIGH) + (sums[n] + sums[n + 1])[None, :]
    flows = lax.psum_scatter(part, "bus", scatter_dimension=0, tiled=True)
    rating = line_rating.astype(jnp.float32) * 0.01
    own_normals = lax.dynamic_slice_in_dim(draws, z * block_rows, block_rows, 0)
    likelihood = jnp.exp(-jnp.dot(own_normals, proposal_mean, precision=HIGHEST))
    share = jnp.sum(jax.nn.softplus(SHARP * (jnp.abs(flows) / rating[None, :] - 1.0)), axis=1)
    overload = lax.psum(share, "line") / SHARP / lines_total
    emphasis = likelihood * overload
    moved_part = jnp.dot(emphasis, own_normals, precision=HIGHEST)
    moved, total = lax.psum((moved_part, jnp.sum(emphasis)), "bus")
    return (flows, overload, scenarios * emphasis / total, proposal_mean + moved / total)


def solution(mesh):
    return jax.shard_map(
        per_device,
        mesh=mesh,
        in_specs=(P("line", "bus"), P("bus"), P("bus"), P("bus"), P("line"), P(), P(), P(), P()),
        out_specs=(P("bus", "line"), P("bus"), P("bus"), P()),
        check_vma=False,
    )
```

```python
import math

import jax
import jax.numpy as jnp
from jax import lax
from jax.experimental import pallas as pl
from jax.experimental.pallas import tpu as pltpu
from jax.sharding import PartitionSpec as P

POINTS = 128
SHARP = 8.0
HIGH = lax.Precision.HIGH
HIGHEST = lax.Precision.HIGHEST
NT = (((1,), (1,)), ((), ()))
NN = (((1,), (0,)), ((), ()))
LANES = 128
EXTRA = 16
MIB = 2**20
CENTRAL = (
    2.81022636e-08, 3.43273939e-07, -3.5233877e-06, -4.39150654e-06, 0.00021858087,
    -0.00125372503, -0.00417768164, 0.246640727, 1.50140941,
)
TAIL = (
    -0.000200214257, 0.000100950558, 0.00134934322, -0.00367342844, 0.00573950773,
    -0.0076224613, 0.00943887047, 1.00167406, 2.83297682,
)


def dot(a, b, dims, precision):
    return lax.dot_general(a, b, dims, precision=precision, preferred_element_type=jnp.float32)


def normal_of(digits):
    x = (2 * (digits >> 7) + 1).astype(jnp.float32) * (2.0 / 16777216.0) - 1.0
    w = -jnp.log((1.0 - x) * (1.0 + x))
    central = w < 5.0
    w = jnp.where(central, w - 2.5, jnp.sqrt(w) - 3.0)
    p = jnp.where(central, CENTRAL[0], TAIL[0])
    for a, b in zip(CENTRAL[1:], TAIL[1:]):
        p = jnp.where(central, a, b) + p * w
    return math.sqrt(2.0) * (p * x)


def block_normals(directions, shifts, start, rows):
    group = min(rows, POINTS)
    n = directions.shape[1]
    digits = jnp.zeros((1, n), jnp.int32)
    bits = group.bit_length() - 1
    lead = min(bits, 3)
    at = lax.broadcasted_iota(jnp.int32, (2**lead, n), 0)
    digits = jnp.zeros((2**lead, n), jnp.int32)
    for b in range(lead):
        digits = digits ^ jnp.where((at >> b & 1) == 1, directions[b : b + 1, :], 0)
    for b in range(lead, bits):
        digits = jnp.concatenate([digits, digits ^ directions[b : b + 1, :]], 0)
    pieces = []
    for j in range(rows // group):
        first = start + j * group
        point = lax.rem(first, POINTS)
        flip = shifts[pl.ds(lax.div(first, POINTS), 1), :]
        for b in range(bits, POINTS.bit_length() - 1):
            flip = flip ^ (directions[b : b + 1, :] * (point >> b & 1))
        pieces.append(normal_of(digits ^ flip))
    return jnp.concatenate(pieces, 0) if len(pieces) > 1 else pieces[0]


def block_width(buses):
    for width in (6272, 3584, 1792, 896, 512, 256):
        if buses % width == 0:
            return width
    return LANES


def head(blocks, ptdf, base, gain, factor, directions, shifts, chol, mean, block_rows):
    lines, buses = ptdf.shape
    n = directions.shape[1]
    width = block_width(buses)
    steps, rows, per = buses // width, buses // LANES, width // LANES

    def body(
        blocks_s, p_h, b_h, g_h, f_h, d_h, s_h, c_h, m_h,
        sums, part, p_v, b_v, g_v, f_v, d_v, s_v, c_v, m_v, p_sem, v_sem,
    ):
        pairs = ((d_h, d_v), (s_h, s_v), (c_h, c_v), (m_h, m_v), (f_h, f_v), (g_h, g_v), (b_h, b_v))
        small = [pltpu.make_async_copy(h, v, v_sem.at[i]) for i, (h, v) in enumerate(pairs)]
        for copy in small:
            copy.start()

        def block_copy(k):
            at = pl.ds(pl.multiple_of(k * width, width), width)
            return pltpu.make_async_copy(p_h.at[:, at], p_v.at[:, at], p_sem.at[k])

        def start(k, _):
            block_copy(k).start()
            return 0

        lax.fori_loop(0, steps, start, 0)
        sums[...] = jnp.zeros_like(sums)
        for copy in small[:2]:
            copy.wait()
        draws = block_normals(d_v, s_v, blocks_s[0] * block_rows, block_rows)
        for copy in small[2:]:
            copy.wait()
        factors = dot(draws + m_v[...], c_v[...], NT, HIGH)

        def step(k, _):
            block_copy(k).wait()

            def row(v):
                return jnp.concatenate([v[pl.ds(k * per + j, 1), :] for j in range(per)], 1)

            g = row(g_v)
            p = p_v[:, pl.ds(pl.multiple_of(k * width, width), width)]
            scaled = (p.astype(jnp.float32) * g).astype(jnp.bfloat16)
            own = lax.broadcasted_iota(jnp.int16, (n, width), 0) == row(f_v).astype(jnp.int16)
            hot = jnp.where(own, jnp.bfloat16(1), jnp.bfloat16(0))
            ratio = row(b_v) / g
            high = ratio.astype(jnp.bfloat16)
            low = (ratio - high.astype(jnp.float32)).astype(jnp.bfloat16)
            rest = jnp.zeros((EXTRA - 2, width), jnp.bfloat16)
            left = jnp.concatenate([hot, high, low, rest], 0)
            sums[...] += lax.dot_general(left, scaled, NT, preferred_element_type=jnp.float32)
            return 0

        lax.fori_loop(0, steps, step, 0)
        base_row = sums[n : n + 1, :] + sums[n + 1 : n + 2, :]
        part[...] = dot(factors, sums[:n, :], NN, HIGH) + base_row

    hbm = pl.BlockSpec(memory_space=pltpu.HBM)
    vmem = pl.BlockSpec(memory_space=pltpu.VMEM)
    return pl.pallas_call(
        body,
        in_specs=[pl.BlockSpec(memory_space=pltpu.SMEM)] + [hbm] * 8,
        out_specs=[vmem, vmem],
        out_shape=[
            jax.ShapeDtypeStruct((n + EXTRA, lines), jnp.float32),
            jax.ShapeDtypeStruct((block_rows, lines), jnp.float32),
        ],
        scratch_shapes=[
            pltpu.VMEM((lines, buses), jnp.bfloat16),
            pltpu.VMEM((rows, LANES), jnp.float32),
            pltpu.VMEM((rows, LANES), jnp.float32),
            pltpu.VMEM((rows, LANES), jnp.int32),
            pltpu.VMEM(directions.shape, jnp.int32),
            pltpu.VMEM(shifts.shape, jnp.int32),
            pltpu.VMEM(chol.shape, jnp.float32),
            pltpu.VMEM((1, n), jnp.float32),
            pltpu.SemaphoreType.DMA((steps,)),
            pltpu.SemaphoreType.DMA((7,)),
        ],
        compiler_params=pltpu.CompilerParams(vmem_limit_bytes=48 * MIB),
        cost_estimate=pl.CostEstimate(
            flops=2 * lines * buses * n, bytes_accessed=2 * lines * buses, transcendentals=0
        ),
        name="segment_sums",
    )(
        blocks,
        *(
            pltpu.with_memory_space_constraint(x, pltpu.HBM)
            for x in (
                ptdf, base.reshape(rows, LANES), gain.reshape(rows, LANES), factor.reshape(rows, LANES),
                directions, shifts, chol, mean.reshape(1, n),
            )
        ),
    )


def middle_parts(blocks, sums, directions, shifts, chol, mean, block_rows):
    n = directions.shape[1]
    lines = sums.shape[1]

    def body(blocks_s, sums_v, d_v, s_v, c_v, m_v, part_2, part_1):
        base_row = sums_v[n : n + 1, :] + sums_v[n + 1 : n + 2, :]
        for i, part in ((2, part_2), (1, part_1)):
            draws = block_normals(d_v, s_v, blocks_s[i] * block_rows, block_rows)
            factors = dot(draws + m_v[...], c_v[...], NT, HIGH)
            part[...] = dot(factors, sums_v[:n, :], NN, HIGH) + base_row

    vmem = pl.BlockSpec(memory_space=pltpu.VMEM)
    return pl.pallas_call(
        body,
        in_specs=[pl.BlockSpec(memory_space=pltpu.SMEM)] + [vmem] * 5,
        out_specs=[vmem] * 2,
        out_shape=[jax.ShapeDtypeStruct((block_rows, lines), jnp.float32)] * 2,
        compiler_params=pltpu.CompilerParams(vmem_limit_bytes=32 * MIB),
        cost_estimate=pl.CostEstimate(
            flops=12 * block_rows * n * (n + lines), bytes_accessed=3 * MIB, transcendentals=4 * block_rows * n
        ),
        name="middle_parts",
    )(blocks, sums, directions, shifts, chol, mean.reshape(1, n))


def own_part(third, blocks, sums, directions, shifts, chol, mean, block_rows):
    n = directions.shape[1]
    lines = sums.shape[1]

    def body(third_h, blocks_s, sums_v, d_v, s_v, c_v, m_v, part, draws, likelihood):
        base_row = sums_v[n : n + 1, :] + sums_v[n + 1 : n + 2, :]
        draws[...] = block_normals(d_v, s_v, blocks_s[3] * block_rows, block_rows)
        factors = dot(draws[...] + m_v[...], c_v[...], NT, HIGH)
        part[...] = dot(factors, sums_v[:n, :], NN, HIGH) + base_row
        tilt = dot(jnp.broadcast_to(m_v[...], (8, n)), draws[...], NT, HIGHEST)
        likelihood[...] = jnp.exp(-tilt)

    vmem = pl.BlockSpec(memory_space=pltpu.VMEM)
    shapes = [(block_rows, lines), (block_rows, n), (8, block_rows)]
    return pl.pallas_call(
        body,
        in_specs=[pl.BlockSpec(memory_space=pl.ANY), pl.BlockSpec(memory_space=pltpu.SMEM)] + [vmem] * 5,
        out_specs=[vmem] * 3,
        out_shape=[jax.ShapeDtypeStruct(s, jnp.float32) for s in shapes],
        compiler_params=pltpu.CompilerParams(vmem_limit_bytes=32 * MIB),
        cost_estimate=pl.CostEstimate(
            flops=6 * block_rows * n * (n + lines), bytes_accessed=2 * MIB, transcendentals=2 * block_rows * n
        ),
        name="own_part",
    )(third, blocks, sums, directions, shifts, chol, mean.reshape(1, n))


def finish_flows(mine, far, beside, rating, draws, likelihood, lines_total):
    rows, lines = mine.shape
    n = draws.shape[1]
    packed_rows = -(-(rows // LANES + n // LANES + 1) // 8) * 8

    def body(mine_v, far_v, beside_v, rating_v, draws_v, like_v, flows, packed):
        value = mine_v[...] + far_v[...] + beside_v[...]
        flows[...] = value
        limit = jnp.concatenate([rating_v[j : j + 1, :] for j in range(lines // LANES)], 1)
        over = jnp.abs(value) * (SHARP / (limit.astype(jnp.float32) * 0.01)) - SHARP
        soft = jnp.maximum(over, 0.0) + jnp.log(1.0 + jnp.exp(-jnp.abs(over)))
        share = dot(jnp.ones((8, lines), jnp.float32), soft, NT, HIGH) * (1.0 / SHARP / lines_total)
        emphasis = like_v[...] * share
        moved = dot(emphasis, draws_v[...], NN, HIGH)
        total = jnp.sum(emphasis[:1, :], axis=1, keepdims=True)
        parts = [share[:1, j * LANES : (j + 1) * LANES] for j in range(rows // LANES)]
        parts += [moved[:1, j * LANES : (j + 1) * LANES] for j in range(n // LANES)]
        parts += [jnp.broadcast_to(total, (1, LANES))]
        parts += [jnp.zeros((1, LANES), jnp.float32)] * (packed_rows - len(parts))
        packed[...] = jnp.concatenate(parts, 0)

    vmem = pl.BlockSpec(memory_space=pltpu.VMEM)
    return pl.pallas_call(
        body,
        in_specs=[vmem] * 6,
        out_specs=[vmem] * 2,
        out_shape=[
            jax.ShapeDtypeStruct((rows, lines), jnp.float32),
            jax.ShapeDtypeStruct((packed_rows, LANES), jnp.float32),
        ],
        compiler_params=pltpu.CompilerParams(vmem_limit_bytes=32 * MIB),
        name="finish_flows",
    )(mine, far, beside, rating.reshape(lines // LANES, LANES), draws, likelihood)


def last_outputs(own, half, other, likelihood, mean, scenarios):
    rows, n = likelihood.shape[1], mean.shape[0]
    a, b = rows // LANES, n // LANES

    def body(own_v, half_v, other_v, like_v, mean_v, overload, weight, new_mean):
        mine = own_v[:a, :]
        everyone = half_v[...] + other_v[...]
        total = everyone[a + b : a + b + 1, :]
        like = jnp.concatenate([like_v[:1, j * LANES : (j + 1) * LANES] for j in range(a)], 0)
        overload[...] = mine
        weight[...] = scenarios * like * mine / total
        new_mean[...] = mean_v[...] + everyone[a : a + b, :] / total

    vmem = pl.BlockSpec(memory_space=pltpu.VMEM)
    shapes = [(a, LANES), (a, LANES), (b, LANES)]
    out = pl.pallas_call(
        body,
        in_specs=[vmem] * 5,
        out_specs=[vmem] * 3,
        out_shape=[jax.ShapeDtypeStruct(s, jnp.float32) for s in shapes],
        name="last_outputs",
    )(own, half, other, likelihood, mean.reshape(b, LANES))
    return [x.reshape(-1) for x in out]


def exchange(value, line_flip, bus_flip):
    lines, buses = lax.axis_size("line"), lax.axis_size("bus")
    pairs = [
        (i * buses + j, (i ^ line_flip) * buses + (j ^ bus_flip))
        for i in range(lines)
        for j in range(buses)
    ]
    return lax.ppermute(value, ("line", "bus"), pairs)


def normals(directions, shifts):
    point = jnp.arange(POINTS, dtype=jnp.int32)
    digits = jnp.zeros((POINTS, directions.shape[1]), jnp.int32)
    for b in range(POINTS.bit_length() - 1):
        digits = digits ^ (point >> b & 1)[:, None] * directions[b][None, :]
    return normal_of(digits[None, :, :] ^ shifts[:, None, :]).reshape(-1, directions.shape[1])


def per_device(
    ptdf,
    base_injection,
    injection_gain,
    factor_of_bus,
    line_rating,
    directions,
    shifts,
    chol_factor,
    proposal_mean,
):
    bus_devices = lax.axis_size("bus")
    lines_total = ptdf.shape[0] * lax.axis_size("line")
    n = directions.shape[1]
    scenarios = POINTS * shifts.shape[0]
    block_rows = scenarios // bus_devices
    z = lax.axis_index("bus").astype(jnp.int32)
    blocks = jnp.stack([z ^ 2, z ^ 3, z ^ 1, z]) if bus_devices == 4 else jnp.stack([z] * 4)
    drawn = (directions, shifts, chol_factor, proposal_mean)
    sums, first = head(
        blocks, ptdf, base_injection, injection_gain, factor_of_bus, *drawn, block_rows
    )

    if bus_devices == 4:
        from_near = exchange(first, 0, 1)
        third, second = middle_parts(blocks, sums, *drawn, block_rows)
        beside = exchange(third, 0, 1)
        mine, own_normals, likelihood = own_part(third, blocks, sums, *drawn, block_rows)
        far = exchange(second + from_near, 0, 3)
        flows, packed = finish_flows(
            mine, far, beside, line_rating, own_normals, likelihood, lines_total
        )
        packed = packed + exchange(packed, 1, 0)
        flip = 2
        while flip < lax.axis_size("line"):
            packed = packed + exchange(packed, flip + 1, 0)
            flip *= 2
        half = packed + exchange(packed, 1, 1)
        overload, weight, new_mean = last_outputs(
            packed, half, exchange(half, 1, 2), likelihood, proposal_mean, scenarios
        )
        return (flows, overload, weight, new_mean)

    draws = normals(directions, shifts)
    factors = dot(draws + proposal_mean[None, :], chol_factor, NT, HIGH)
    part = dot(factors, sums[:n], NN, HIGH) + (sums[n] + sums[n + 1])[None, :]
    flows = lax.psum_scatter(part, "bus", scatter_dimension=0, tiled=True)
    rating = line_rating.astype(jnp.float32) * 0.01
    own_normals = lax.dynamic_slice_in_dim(draws, z * block_rows, block_rows, 0)
    likelihood = jnp.exp(-jnp.dot(own_normals, proposal_mean, precision=HIGHEST))
    share = jnp.sum(jax.nn.softplus(SHARP * (jnp.abs(flows) / rating[None, :] - 1.0)), axis=1)
    overload = lax.psum(share, "line") / SHARP / lines_total
    emphasis = likelihood * overload
    moved_part = jnp.dot(emphasis, own_normals, precision=HIGHEST)
    moved, total = lax.psum((moved_part, jnp.sum(emphasis)), "bus")
    return (flows, overload, scenarios * emphasis / total, proposal_mean + moved / total)


def solution(mesh):
    return jax.shard_map(
        per_device,
        mesh=mesh,
        in_specs=(P("line", "bus"), P("bus"), P("bus"), P("bus"), P("line"), P(), P(), P(), P()),
        out_specs=(P("bus", "line"), P("bus"), P("bus"), P()),
        check_vma=False,
    )
```

```python
import math

import jax
import jax.numpy as jnp
from jax import lax
from jax.experimental import pallas as pl
from jax.experimental.pallas import tpu as pltpu
from jax.sharding import PartitionSpec as P

POINTS = 128
SHARP = 8.0
HIGH = lax.Precision.HIGH
HIGHEST = lax.Precision.HIGHEST
NT = (((1,), (1,)), ((), ()))
NN = (((1,), (0,)), ((), ()))
LANES = 128
EXTRA = 16
MIB = 2**20
CENTRAL = (
    2.81022636e-08, 3.43273939e-07, -3.5233877e-06, -4.39150654e-06, 0.00021858087,
    -0.00125372503, -0.00417768164, 0.246640727, 1.50140941,
)
TAIL = (
    -0.000200214257, 0.000100950558, 0.00134934322, -0.00367342844, 0.00573950773,
    -0.0076224613, 0.00943887047, 1.00167406, 2.83297682,
)


def dot(a, b, dims, precision):
    return lax.dot_general(a, b, dims, precision=precision, preferred_element_type=jnp.float32)


def normal_of(digits):
    x = (2 * (digits >> 7) + 1).astype(jnp.float32) * (2.0 / 16777216.0) - 1.0
    w = -jnp.log((1.0 - x) * (1.0 + x))
    central = w < 5.0
    w = jnp.where(central, w - 2.5, jnp.sqrt(w) - 3.0)
    p = jnp.where(central, CENTRAL[0], TAIL[0])
    for a, b in zip(CENTRAL[1:], TAIL[1:]):
        p = jnp.where(central, a, b) + p * w
    return math.sqrt(2.0) * (p * x)


def block_normals(directions, shifts, start, rows):
    group = min(rows, POINTS)
    n = directions.shape[1]
    digits = jnp.zeros((1, n), jnp.int32)
    bits = group.bit_length() - 1
    lead = min(bits, 3)
    at = lax.broadcasted_iota(jnp.int32, (2**lead, n), 0)
    digits = jnp.zeros((2**lead, n), jnp.int32)
    for b in range(lead):
        digits = digits ^ jnp.where((at >> b & 1) == 1, directions[b : b + 1, :], 0)
    for b in range(lead, bits):
        digits = jnp.concatenate([digits, digits ^ directions[b : b + 1, :]], 0)
    pieces = []
    for j in range(rows // group):
        first = start + j * group
        point = lax.rem(first, POINTS)
        flip = shifts[pl.ds(lax.div(first, POINTS), 1), :]
        for b in range(bits, POINTS.bit_length() - 1):
            flip = flip ^ (directions[b : b + 1, :] * (point >> b & 1))
        pieces.append(normal_of(digits ^ flip))
    return jnp.concatenate(pieces, 0) if len(pieces) > 1 else pieces[0]


def block_width(buses):
    for width in (6272, 3584, 1792, 896, 512, 256):
        if buses % width == 0:
            return width
    return LANES


def head(blocks, ptdf, base, gain, factor, directions, shifts, chol, mean, block_rows):
    lines, buses = ptdf.shape
    n = directions.shape[1]
    width = block_width(buses)
    steps, rows, per = buses // width, buses // LANES, width // LANES

    def body(
        blocks_s, p_h, b_h, g_h, f_h, d_h, s_h, c_h, m_h,
        sums, part, p_v, b_v, g_v, f_v, d_v, s_v, c_v, m_v, p_sem, v_sem,
    ):
        pairs = ((d_h, d_v), (s_h, s_v), (c_h, c_v), (m_h, m_v), (f_h, f_v), (g_h, g_v), (b_h, b_v))
        small = [pltpu.make_async_copy(h, v, v_sem.at[i]) for i, (h, v) in enumerate(pairs)]
        for copy in small:
            copy.start()

        def block_copy(k):
            at = pl.ds(pl.multiple_of(k * width, width), width)
            return pltpu.make_async_copy(p_h.at[:, at], p_v.at[:, at], p_sem.at[k])

        def start(k, _):
            block_copy(k).start()
            return 0

        lax.fori_loop(0, steps, start, 0)
        sums[...] = jnp.zeros_like(sums)
        for copy in small[:2]:
            copy.wait()
        draws = block_normals(d_v, s_v, blocks_s[0] * block_rows, block_rows)
        for copy in small[2:]:
            copy.wait()
        factors = dot(draws + m_v[...], c_v[...], NT, HIGH)

        def step(k, _):
            block_copy(k).wait()

            def row(v):
                return jnp.concatenate([v[pl.ds(k * per + j, 1), :] for j in range(per)], 1)

            g = row(g_v)
            p = p_v[:, pl.ds(pl.multiple_of(k * width, width), width)]
            scaled = (p.astype(jnp.float32) * g).astype(jnp.bfloat16)
            own = lax.broadcasted_iota(jnp.int16, (n, width), 0) == row(f_v).astype(jnp.int16)
            hot = jnp.where(own, jnp.bfloat16(1), jnp.bfloat16(0))
            ratio = row(b_v) / g
            high = ratio.astype(jnp.bfloat16)
            low = (ratio - high.astype(jnp.float32)).astype(jnp.bfloat16)
            rest = jnp.zeros((EXTRA - 2, width), jnp.bfloat16)
            left = jnp.concatenate([hot, high, low, rest], 0)
            sums[...] += lax.dot_general(left, scaled, NT, preferred_element_type=jnp.float32)
            return 0

        lax.fori_loop(0, steps, step, 0)
        base_row = sums[n : n + 1, :] + sums[n + 1 : n + 2, :]
        part[...] = dot(factors, sums[:n, :], NN, HIGH) + base_row

    hbm = pl.BlockSpec(memory_space=pltpu.HBM)
    vmem = pl.BlockSpec(memory_space=pltpu.VMEM)
    return pl.pallas_call(
        body,
        in_specs=[pl.BlockSpec(memory_space=pltpu.SMEM)] + [hbm] * 8,
        out_specs=[vmem, vmem],
        out_shape=[
            jax.ShapeDtypeStruct((n + EXTRA, lines), jnp.float32),
            jax.ShapeDtypeStruct((block_rows, lines), jnp.float32),
        ],
        scratch_shapes=[
            pltpu.VMEM((lines, buses), jnp.bfloat16),
            pltpu.VMEM((rows, LANES), jnp.float32),
            pltpu.VMEM((rows, LANES), jnp.float32),
            pltpu.VMEM((rows, LANES), jnp.int32),
            pltpu.VMEM(directions.shape, jnp.int32),
            pltpu.VMEM(shifts.shape, jnp.int32),
            pltpu.VMEM(chol.shape, jnp.float32),
            pltpu.VMEM((1, n), jnp.float32),
            pltpu.SemaphoreType.DMA((steps,)),
            pltpu.SemaphoreType.DMA((7,)),
        ],
        compiler_params=pltpu.CompilerParams(vmem_limit_bytes=48 * MIB),
        cost_estimate=pl.CostEstimate(
            flops=2 * lines * buses * n, bytes_accessed=2 * lines * buses, transcendentals=0
        ),
        name="segment_sums",
    )(
        blocks,
        *(
            pltpu.with_memory_space_constraint(x, pltpu.HBM)
            for x in (
                ptdf, base.reshape(rows, LANES), gain.reshape(rows, LANES), factor.reshape(rows, LANES),
                directions, shifts, chol, mean.reshape(1, n),
            )
        ),
    )


def middle_parts(blocks, sums, directions, shifts, chol, mean, block_rows):
    n = directions.shape[1]
    lines = sums.shape[1]

    def body(blocks_s, sums_v, d_v, s_v, c_v, m_v, part_2, part_1):
        base_row = sums_v[n : n + 1, :] + sums_v[n + 1 : n + 2, :]
        for i, part in ((2, part_2), (1, part_1)):
            draws = block_normals(d_v, s_v, blocks_s[i] * block_rows, block_rows)
            factors = dot(draws + m_v[...], c_v[...], NT, HIGH)
            part[...] = dot(factors, sums_v[:n, :], NN, HIGH) + base_row

    vmem = pl.BlockSpec(memory_space=pltpu.VMEM)
    return pl.pallas_call(
        body,
        in_specs=[pl.BlockSpec(memory_space=pltpu.SMEM)] + [vmem] * 5,
        out_specs=[vmem] * 2,
        out_shape=[jax.ShapeDtypeStruct((block_rows, lines), jnp.float32)] * 2,
        compiler_params=pltpu.CompilerParams(vmem_limit_bytes=32 * MIB),
        cost_estimate=pl.CostEstimate(
            flops=12 * block_rows * n * (n + lines), bytes_accessed=3 * MIB, transcendentals=4 * block_rows * n
        ),
        name="middle_parts",
    )(blocks, sums, directions, shifts, chol, mean.reshape(1, n))


def own_part(third, blocks, sums, directions, shifts, chol, mean, block_rows):
    n = directions.shape[1]
    lines = sums.shape[1]

    def body(third_h, blocks_s, sums_v, d_v, s_v, c_v, m_v, part, draws, likelihood):
        base_row = sums_v[n : n + 1, :] + sums_v[n + 1 : n + 2, :]
        draws[...] = block_normals(d_v, s_v, blocks_s[3] * block_rows, block_rows)
        factors = dot(draws[...] + m_v[...], c_v[...], NT, HIGH)
        part[...] = dot(factors, sums_v[:n, :], NN, HIGH) + base_row
        tilt = dot(jnp.broadcast_to(m_v[...], (8, n)), draws[...], NT, HIGHEST)
        likelihood[...] = jnp.exp(-tilt)

    vmem = pl.BlockSpec(memory_space=pltpu.VMEM)
    shapes = [(block_rows, lines), (block_rows, n), (8, block_rows)]
    return pl.pallas_call(
        body,
        in_specs=[pl.BlockSpec(memory_space=pl.ANY), pl.BlockSpec(memory_space=pltpu.SMEM)] + [vmem] * 5,
        out_specs=[vmem] * 3,
        out_shape=[jax.ShapeDtypeStruct(s, jnp.float32) for s in shapes],
        compiler_params=pltpu.CompilerParams(vmem_limit_bytes=32 * MIB),
        cost_estimate=pl.CostEstimate(
            flops=6 * block_rows * n * (n + lines), bytes_accessed=2 * MIB, transcendentals=2 * block_rows * n
        ),
        name="own_part",
    )(third, blocks, sums, directions, shifts, chol, mean.reshape(1, n))


def overload_sums(mine, far, beside, rating, draws, likelihood, lines_total):
    rows, lines = mine.shape
    n = draws.shape[1]
    packed_rows = -(-(rows // LANES + n // LANES + 1) // 8) * 8

    def body(mine_v, far_v, beside_v, rating_v, draws_v, like_v, packed):
        value = mine_v[...] + far_v[...] + beside_v[...]
        limit = jnp.concatenate([rating_v[j : j + 1, :] for j in range(lines // LANES)], 1)
        over = jnp.abs(value) * (SHARP / (limit.astype(jnp.float32) * 0.01)) - SHARP
        soft = jnp.maximum(over, 0.0) + jnp.log(1.0 + jnp.exp(-jnp.abs(over)))
        share = dot(jnp.ones((8, lines), jnp.float32), soft, NT, HIGH) * (1.0 / SHARP / lines_total)
        emphasis = like_v[...] * share
        moved = dot(emphasis, draws_v[...], NN, HIGH)
        total = jnp.sum(emphasis[:1, :], axis=1, keepdims=True)
        parts = [share[:1, j * LANES : (j + 1) * LANES] for j in range(rows // LANES)]
        parts += [moved[:1, j * LANES : (j + 1) * LANES] for j in range(n // LANES)]
        parts += [jnp.broadcast_to(total, (1, LANES))]
        parts += [jnp.zeros((1, LANES), jnp.float32)] * (packed_rows - len(parts))
        packed[...] = jnp.concatenate(parts, 0)

    vmem = pl.BlockSpec(memory_space=pltpu.VMEM)
    return pl.pallas_call(
        body,
        in_specs=[vmem] * 6,
        out_specs=vmem,
        out_shape=jax.ShapeDtypeStruct((packed_rows, LANES), jnp.float32),
        compiler_params=pltpu.CompilerParams(vmem_limit_bytes=32 * MIB),
        name="overload_sums",
    )(mine, far, beside, rating.reshape(lines // LANES, LANES), draws, likelihood)


def last_outputs(own, half, other, likelihood, mean, scenarios):
    rows, n = likelihood.shape[1], mean.shape[0]
    a, b = rows // LANES, n // LANES

    def body(own_v, half_v, other_v, like_v, mean_v, overload, weight, new_mean):
        mine = own_v[:a, :]
        everyone = half_v[...] + other_v[...]
        total = everyone[a + b : a + b + 1, :]
        like = jnp.concatenate([like_v[:1, j * LANES : (j + 1) * LANES] for j in range(a)], 0)
        overload[...] = mine
        weight[...] = scenarios * like * mine / total
        new_mean[...] = mean_v[...] + everyone[a : a + b, :] / total

    vmem = pl.BlockSpec(memory_space=pltpu.VMEM)
    shapes = [(a, LANES), (a, LANES), (b, LANES)]
    out = pl.pallas_call(
        body,
        in_specs=[vmem] * 5,
        out_specs=[vmem] * 3,
        out_shape=[jax.ShapeDtypeStruct(s, jnp.float32) for s in shapes],
        compiler_params=pltpu.CompilerParams(vmem_limit_bytes=8 * MIB),
        name="last_outputs",
    )(own, half, other, likelihood, mean.reshape(b, LANES))
    return [x.reshape(-1) for x in out]


def exchange(value, line_flip, bus_flip):
    lines, buses = lax.axis_size("line"), lax.axis_size("bus")
    pairs = [
        (i * buses + j, (i ^ line_flip) * buses + (j ^ bus_flip))
        for i in range(lines)
        for j in range(buses)
    ]
    return lax.ppermute(value, ("line", "bus"), pairs)


def normals(directions, shifts):
    point = jnp.arange(POINTS, dtype=jnp.int32)
    digits = jnp.zeros((POINTS, directions.shape[1]), jnp.int32)
    for b in range(POINTS.bit_length() - 1):
        digits = digits ^ (point >> b & 1)[:, None] * directions[b][None, :]
    return normal_of(digits[None, :, :] ^ shifts[:, None, :]).reshape(-1, directions.shape[1])


def per_device(
    ptdf,
    base_injection,
    injection_gain,
    factor_of_bus,
    line_rating,
    directions,
    shifts,
    chol_factor,
    proposal_mean,
):
    bus_devices = lax.axis_size("bus")
    lines_total = ptdf.shape[0] * lax.axis_size("line")
    n = directions.shape[1]
    scenarios = POINTS * shifts.shape[0]
    block_rows = scenarios // bus_devices
    z = lax.axis_index("bus").astype(jnp.int32)
    blocks = jnp.stack([z ^ 2, z ^ 3, z ^ 1, z]) if bus_devices == 4 else jnp.stack([z] * 4)
    drawn = (directions, shifts, chol_factor, proposal_mean)
    sums, first = head(
        blocks, ptdf, base_injection, injection_gain, factor_of_bus, *drawn, block_rows
    )

    if bus_devices == 4:
        from_near = exchange(first, 0, 1)
        third, second = middle_parts(blocks, sums, *drawn, block_rows)
        beside = exchange(third, 0, 1)
        mine, own_normals, likelihood = own_part(third, blocks, sums, *drawn, block_rows)
        far = exchange(second + from_near, 0, 3)
        packed = overload_sums(
            mine, far, beside, line_rating, own_normals, likelihood, lines_total
        )
        flows = mine + far + beside
        packed = packed + exchange(packed, 1, 0)
        flip = 2
        while flip < lax.axis_size("line"):
            packed = packed + exchange(packed, flip + 1, 0)
            flip *= 2
        half = packed + exchange(packed, 1, 1)
        overload, weight, new_mean = last_outputs(
            packed, half, exchange(half, 1, 2), likelihood, proposal_mean, scenarios
        )
        return (flows, overload, weight, new_mean)

    draws = normals(directions, shifts)
    factors = dot(draws + proposal_mean[None, :], chol_factor, NT, HIGH)
    part = dot(factors, sums[:n], NN, HIGH) + (sums[n] + sums[n + 1])[None, :]
    flows = lax.psum_scatter(part, "bus", scatter_dimension=0, tiled=True)
    rating = line_rating.astype(jnp.float32) * 0.01
    own_normals = lax.dynamic_slice_in_dim(draws, z * block_rows, block_rows, 0)
    likelihood = jnp.exp(-jnp.dot(own_normals, proposal_mean, precision=HIGHEST))
    share = jnp.sum(jax.nn.softplus(SHARP * (jnp.abs(flows) / rating[None, :] - 1.0)), axis=1)
    overload = lax.psum(share, "line") / SHARP / lines_total
    emphasis = likelihood * overload
    moved_part = jnp.dot(emphasis, own_normals, precision=HIGHEST)
    moved, total = lax.psum((moved_part, jnp.sum(emphasis)), "bus")
    return (flows, overload, scenarios * emphasis / total, proposal_mean + moved / total)


def solution(mesh):
    return jax.shard_map(
        per_device,
        mesh=mesh,
        in_specs=(P("line", "bus"), P("bus"), P("bus"), P("bus"), P("line"), P(), P(), P(), P()),
        out_specs=(P("bus", "line"), P("bus"), P("bus"), P()),
        check_vma=False,
    )
```

```python
import math

import jax
import jax.numpy as jnp
from jax import lax
from jax.experimental import pallas as pl
from jax.experimental.pallas import tpu as pltpu
from jax.sharding import PartitionSpec as P

POINTS = 128
SHARP = 8.0
HIGH = lax.Precision.HIGH
HIGHEST = lax.Precision.HIGHEST
NT = (((1,), (1,)), ((), ()))
NN = (((1,), (0,)), ((), ()))
LANES = 128
EXTRA = 16
QUARTERS = 4
MIB = 2**20
CENTRAL = (
    2.81022636e-08, 3.43273939e-07, -3.5233877e-06, -4.39150654e-06, 0.00021858087,
    -0.00125372503, -0.00417768164, 0.246640727, 1.50140941,
)
TAIL = (
    -0.000200214257, 0.000100950558, 0.00134934322, -0.00367342844, 0.00573950773,
    -0.0076224613, 0.00943887047, 1.00167406, 2.83297682,
)


def dot(a, b, dims, precision):
    return lax.dot_general(a, b, dims, precision=precision, preferred_element_type=jnp.float32)


def normal_of(digits):
    x = (2 * (digits >> 7) + 1).astype(jnp.float32) * (2.0 / 16777216.0) - 1.0
    w = -jnp.log((1.0 - x) * (1.0 + x))
    central = w < 5.0
    w = jnp.where(central, w - 2.5, jnp.sqrt(w) - 3.0)
    p = jnp.where(central, CENTRAL[0], TAIL[0])
    for a, b in zip(CENTRAL[1:], TAIL[1:]):
        p = jnp.where(central, a, b) + p * w
    return math.sqrt(2.0) * (p * x)


def block_normals(directions, shifts, start, rows):
    group = min(rows, POINTS)
    n = directions.shape[1]
    digits = jnp.zeros((1, n), jnp.int32)
    bits = group.bit_length() - 1
    lead = min(bits, 3)
    at = lax.broadcasted_iota(jnp.int32, (2**lead, n), 0)
    digits = jnp.zeros((2**lead, n), jnp.int32)
    for b in range(lead):
        digits = digits ^ jnp.where((at >> b & 1) == 1, directions[b : b + 1, :], 0)
    for b in range(lead, bits):
        digits = jnp.concatenate([digits, digits ^ directions[b : b + 1, :]], 0)
    pieces = []
    for j in range(rows // group):
        first = start + j * group
        point = lax.rem(first, POINTS)
        flip = shifts[pl.ds(lax.div(first, POINTS), 1), :]
        for b in range(bits, POINTS.bit_length() - 1):
            flip = flip ^ (directions[b : b + 1, :] * (point >> b & 1))
        pieces.append(normal_of(digits ^ flip))
    return jnp.concatenate(pieces, 0) if len(pieces) > 1 else pieces[0]


def block_width(buses):
    for width in (6272, 3584, 1792, 896, 512, 256):
        if buses % width == 0:
            return width
    return LANES


def head(blocks, ptdf, base, gain, factor, n):
    lines, buses = ptdf.shape
    width = block_width(buses)
    steps, rows, per = buses // width, buses // LANES, width // LANES
    q, groups = lines // QUARTERS, n // LANES

    def body(
        blocks_s, p_h, b_h, g_h, f_h, out_0, out_1, out_2, out_3,
        sums, flipped, base_v, p_v, b_v, g_v, f_v, p_sem, v_sem,
    ):
        pairs = ((f_h, f_v), (g_h, g_v), (b_h, b_v))
        small = [pltpu.make_async_copy(h, v, v_sem.at[i]) for i, (h, v) in enumerate(pairs)]
        for copy in small:
            copy.start()

        def block_copy(k):
            at = pl.ds(pl.multiple_of(k * width, width), width)
            return pltpu.make_async_copy(p_h.at[:, at], p_v.at[:, at], p_sem.at[k])

        def start(k, _):
            block_copy(k).start()
            return 0

        lax.fori_loop(0, steps, start, 0)
        sums[...] = jnp.zeros_like(sums)
        for copy in small:
            copy.wait()

        def step(k, _):
            block_copy(k).wait()

            def row(v):
                return jnp.concatenate([v[pl.ds(k * per + j, 1), :] for j in range(per)], 1)

            g = row(g_v)
            p = p_v[:, pl.ds(pl.multiple_of(k * width, width), width)]
            scaled = (p.astype(jnp.float32) * g).astype(jnp.bfloat16)
            own = lax.broadcasted_iota(jnp.int16, (n, width), 0) == row(f_v).astype(jnp.int16)
            hot = jnp.where(own, jnp.bfloat16(1), jnp.bfloat16(0))
            ratio = row(b_v) / g
            high = ratio.astype(jnp.bfloat16)
            low = (ratio - high.astype(jnp.float32)).astype(jnp.bfloat16)
            rest = jnp.zeros((EXTRA - 2, width), jnp.bfloat16)
            left = jnp.concatenate([hot, high, low, rest], 0)
            sums[...] += lax.dot_general(left, scaled, NT, preferred_element_type=jnp.float32)
            return 0

        lax.fori_loop(0, steps, step, 0)
        flipped[...] = sums[:n, :].T
        base_row = sums[n : n + 1, :] + sums[n + 1 : n + 2, :]
        blank = jnp.zeros((1, LANES - q), jnp.float32)
        for d in range(QUARTERS):
            base_v[8 * d : 8 * d + 8, :] = jnp.broadcast_to(
                jnp.concatenate([base_row[:, d * q : d * q + q], blank], 1), (8, LANES)
            )
        for i, out in enumerate((out_0, out_1, out_2, out_3)):
            d = blocks_s[i]
            for j in range(groups):
                out[j * q : j * q + q, :] = flipped[
                    pl.ds(pl.multiple_of(d * q, 8), q), j * LANES : (j + 1) * LANES
                ]
            out[groups * q :, :] = base_v[pl.ds(pl.multiple_of(d * 8, 8), 8), :]

    hbm = pl.BlockSpec(memory_space=pltpu.HBM)
    vmem = pl.BlockSpec(memory_space=pltpu.VMEM)
    return pl.pallas_call(
        body,
        in_specs=[pl.BlockSpec(memory_space=pltpu.SMEM)] + [hbm] * 4,
        out_specs=[vmem] * QUARTERS,
        out_shape=[jax.ShapeDtypeStruct((groups * q + 8, LANES), jnp.float32)] * QUARTERS,
        scratch_shapes=[
            pltpu.VMEM((n + EXTRA, lines), jnp.float32),
            pltpu.VMEM((lines, n), jnp.float32),
            pltpu.VMEM((8 * QUARTERS, LANES), jnp.float32),
            pltpu.VMEM((lines, buses), jnp.bfloat16),
            pltpu.VMEM((rows, LANES), jnp.float32),
            pltpu.VMEM((rows, LANES), jnp.float32),
            pltpu.VMEM((rows, LANES), jnp.int32),
            pltpu.SemaphoreType.DMA((steps,)),
            pltpu.SemaphoreType.DMA((3,)),
        ],
        compiler_params=pltpu.CompilerParams(vmem_limit_bytes=48 * MIB),
        cost_estimate=pl.CostEstimate(
            flops=2 * lines * buses * n, bytes_accessed=2 * lines * buses, transcendentals=0
        ),
        name="segment_sums",
    )(
        blocks,
        *(
            pltpu.with_memory_space_constraint(x, pltpu.HBM)
            for x in (
                ptdf, base.reshape(rows, LANES), gain.reshape(rows, LANES), factor.reshape(rows, LANES),
            )
        ),
    )


def split(x):
    high = x.astype(jnp.bfloat16)
    return high, (x - high.astype(jnp.float32)).astype(jnp.bfloat16)


def all_factors(directions, shifts, chol, mean):
    n = directions.shape[1]
    scenarios = POINTS * shifts.shape[0]
    block = 2 * POINTS

    def body(d_v, s_v, c_v, m_v, f_high, f_low, kept, likelihood, c_high, c_low):
        c_high[...], c_low[...] = split(c_v[...])
        mean_terms = jnp.concatenate([*split(m_v[...]), jnp.zeros((14, n), jnp.bfloat16)], 0)

        def step(k, _):
            at = pl.ds(pl.multiple_of(k * block, block), block)
            draws = block_normals(d_v, s_v, k * block, block)
            kept[at, :] = draws
            high, low = split(draws + m_v[...])
            both = dot(jnp.concatenate([high, low], 0), c_high[...], NT, None)
            factors = both[:block, :] + (both[block:, :] + dot(high, c_low[...], NT, None))
            f_high[at, :], f_low[at, :] = split(factors)
            high, low = split(draws)
            tilt = dot(mean_terms, high, NT, None)
            tilt = tilt[:1, :] + (tilt[1:2, :] + dot(mean_terms, low, NT, None)[:1, :])
            for j in range(block // LANES):
                likelihood[pl.ds(k * (block // LANES) + j, 1), :] = jnp.exp(
                    -tilt[:, j * LANES : (j + 1) * LANES]
                )
            return 0

        lax.fori_loop(0, scenarios // block, step, 0)

    vmem = pl.BlockSpec(memory_space=pltpu.VMEM)
    big = jax.ShapeDtypeStruct((scenarios, n), jnp.bfloat16)
    return pl.pallas_call(
        body,
        in_specs=[vmem] * 4,
        out_specs=[vmem] * 4,
        out_shape=[
            big,
            big,
            jax.ShapeDtypeStruct((scenarios, n), jnp.float32),
            jax.ShapeDtypeStruct((scenarios // LANES, LANES), jnp.float32),
        ],
        scratch_shapes=[pltpu.VMEM((n, n), jnp.bfloat16), pltpu.VMEM((n, n), jnp.bfloat16)],
        compiler_params=pltpu.CompilerParams(vmem_limit_bytes=20 * MIB),
        cost_estimate=pl.CostEstimate(
            flops=6 * scenarios * n * n, bytes_accessed=6 * MIB, transcendentals=2 * scenarios * n
        ),
        name="all_factors",
    )(directions, shifts, chol, mean.reshape(1, n))


def pair_sum(mine, other, later):
    def body(mine_v, other_v, later_v, out, passed):
        out[...] = mine_v[...] + other_v[...]
        passed[...] = later_v[...]

    vmem = pl.BlockSpec(memory_space=pltpu.VMEM)
    return pl.pallas_call(
        body,
        in_specs=[vmem] * 3,
        out_specs=[vmem] * 2,
        out_shape=[jax.ShapeDtypeStruct(mine.shape, jnp.float32)] * 2,
        compiler_params=pltpu.CompilerParams(vmem_limit_bytes=4 * MIB),
        name="pair_sum",
    )(mine, other, later)


def quarter_flows(blocks, mine, beside, far, scale, f_high, f_low, lines_total):
    scenarios, n = f_high.shape
    q = scale.shape[0]
    block, groups = scenarios // QUARTERS, n // LANES

    def body(
        blocks_s, mine_v, beside_v, far_v, scale_v, high_v, low_v, out_0, out_1, out_2, out_3, share, flows
    ):
        total = mine_v[...] + beside_v[...] + far_v[...]
        g = jnp.concatenate([total[j * q : j * q + q, :] for j in range(groups)], 1)
        diagonal = lax.broadcasted_iota(jnp.int32, (q, LANES), 0) == lax.broadcasted_iota(
            jnp.int32, (q, LANES), 1
        )
        base = jnp.sum(
            jnp.where(diagonal, total[groups * q : groups * q + 1, :], 0.0), axis=1, keepdims=True
        )
        g_high, g_low = split(g)
        wide = dot(jnp.concatenate([g_high, g_low], 0), high_v[...], NT, None)
        value = wide[:q, :] + (wide[q:, :] + dot(g_high, low_v[...], NT, None)) + base
        flows[...] = value
        over = jnp.abs(value) * jnp.concatenate([scale_v[...]] * (scenarios // LANES), 1) - SHARP
        soft = jnp.maximum(over, 0.0) + jnp.log(1.0 + jnp.exp(-jnp.abs(over)))
        row = jnp.sum(soft, axis=0, keepdims=True) * (1.0 / SHARP / lines_total)
        share[...] = jnp.concatenate(
            [row[:, j * LANES : (j + 1) * LANES] for j in range(scenarios // LANES)], 0
        )
        for i, out in enumerate((out_0, out_1, out_2, out_3)):
            out[...] = flows[:, pl.ds(pl.multiple_of(blocks_s[i] * block, LANES), block)]

    vmem = pl.BlockSpec(memory_space=pltpu.VMEM)
    shapes = [(q, block)] * QUARTERS + [(scenarios // LANES, LANES)]
    return pl.pallas_call(
        body,
        in_specs=[pl.BlockSpec(memory_space=pltpu.SMEM)] + [vmem] * 6,
        out_specs=[vmem] * 5,
        out_shape=[jax.ShapeDtypeStruct(s, jnp.float32) for s in shapes],
        scratch_shapes=[pltpu.VMEM((q, scenarios), jnp.float32)],
        compiler_params=pltpu.CompilerParams(vmem_limit_bytes=12 * MIB),
        name="quarter_flows",
    )(blocks, mine, beside, far, scale, f_high, f_low)


def own_flows(blocks, parts):
    q, block = parts[0].shape

    def body(blocks_s, part_0, part_1, part_2, part_3, out, whole):
        for i, part in enumerate((part_0, part_1, part_2, part_3)):
            whole[pl.ds(pl.multiple_of(blocks_s[i] * q, 8), q), :] = part[...]
        out[...] = whole[...].T

    vmem = pl.BlockSpec(memory_space=pltpu.VMEM)
    return pl.pallas_call(
        body,
        in_specs=[pl.BlockSpec(memory_space=pltpu.SMEM)] + [vmem] * 4,
        out_specs=vmem,
        out_shape=pltpu.HBM((block, q * QUARTERS), jnp.float32),
        scratch_shapes=[pltpu.VMEM((q * QUARTERS, block), jnp.float32)],
        compiler_params=pltpu.CompilerParams(vmem_limit_bytes=4 * MIB),
        name="own_flows",
    )(blocks, *parts)


def last_outputs(after, blocks, half, other, likelihood, draws, mean):
    scenarios, n = draws.shape
    a, b = scenarios // QUARTERS // LANES, n // LANES

    def body(after_h, blocks_s, half_v, other_v, like_v, draws_v, mean_v, overload, weight, new_mean, kept):
        every = half_v[...] + other_v[...]
        emphasis = like_v[...] * every
        total = jnp.sum(jnp.sum(emphasis, axis=1, keepdims=True), axis=0, keepdims=True)
        columns = emphasis.T
        parts = jnp.zeros((8, n), jnp.float32)
        for g in range(scenarios // LANES):
            piece = draws_v[g * LANES : (g + 1) * LANES, :] * columns[:, g : g + 1]
            parts = parts + jnp.sum(piece.reshape(LANES // 8, 8, n), axis=0)
        moved = jnp.sum(parts, axis=0, keepdims=True)
        moved = jnp.concatenate([moved[:, j * LANES : (j + 1) * LANES] for j in range(b)], 0)
        kept[0] = every
        kept[1] = scenarios * emphasis / total
        at = pl.ds(blocks_s[3] * a, a)
        overload[...] = kept[0, at, :]
        weight[...] = kept[1, at, :]
        new_mean[...] = mean_v[...] + moved / total

    vmem = pl.BlockSpec(memory_space=pltpu.VMEM)
    shapes = [(a, LANES), (a, LANES), (b, LANES)]
    out = pl.pallas_call(
        body,
        in_specs=[pl.BlockSpec(memory_space=pl.ANY), pl.BlockSpec(memory_space=pltpu.SMEM)] + [vmem] * 5,
        out_specs=[vmem] * 3,
        out_shape=[jax.ShapeDtypeStruct(s, jnp.float32) for s in shapes],
        scratch_shapes=[pltpu.VMEM((2, scenarios // LANES, LANES), jnp.float32)],
        compiler_params=pltpu.CompilerParams(vmem_limit_bytes=8 * MIB),
        name="last_outputs",
    )(
        pltpu.with_memory_space_constraint(after, pltpu.HBM), blocks, half, other, likelihood, draws,
        mean.reshape(b, LANES),
    )
    return [x.reshape(-1) for x in out]


def exchange(value, line_flip, bus_flip):
    lines, buses = lax.axis_size("line"), lax.axis_size("bus")
    pairs = [
        (i * buses + j, (i ^ line_flip) * buses + (j ^ bus_flip))
        for i in range(lines)
        for j in range(buses)
    ]
    return lax.ppermute(value, ("line", "bus"), pairs)


def normals(directions, shifts):
    point = jnp.arange(POINTS, dtype=jnp.int32)
    digits = jnp.zeros((POINTS, directions.shape[1]), jnp.int32)
    for b in range(POINTS.bit_length() - 1):
        digits = digits ^ (point >> b & 1)[:, None] * directions[b][None, :]
    return normal_of(digits[None, :, :] ^ shifts[:, None, :]).reshape(-1, directions.shape[1])


def per_device(
    ptdf,
    base_injection,
    injection_gain,
    factor_of_bus,
    line_rating,
    directions,
    shifts,
    chol_factor,
    proposal_mean,
):
    bus_devices = lax.axis_size("bus")
    lines = ptdf.shape[0]
    lines_total = lines * lax.axis_size("line")
    n = directions.shape[1]
    scenarios = POINTS * shifts.shape[0]
    z = lax.axis_index("bus").astype(jnp.int32)
    drawn = (directions, shifts, chol_factor, proposal_mean)
    own_buses = (ptdf, base_injection, injection_gain, factor_of_bus)

    if bus_devices == QUARTERS:
        blocks = jnp.stack([z ^ 2, z ^ 3, z ^ 1, z])
        for_pair, for_far, for_near, mine = head(blocks, *own_buses, n)
        from_near = exchange(for_pair, 0, 1)
        f_high, f_low, draws, likelihood = all_factors(*drawn)
        beside = exchange(for_near, 0, 1)
        far = exchange(for_far + from_near, 0, 3)
        q, block = lines // QUARTERS, scenarios // QUARTERS
        rating = lax.dynamic_slice_in_dim(line_rating, z * q, q).astype(jnp.float32) * 0.01
        scale = jnp.broadcast_to((SHARP / rating)[:, None], (q, LANES))
        to_2, to_3, to_1, own, share = quarter_flows(
            blocks, mine, beside, far, scale, f_high, f_low, lines_total
        )
        from_2 = exchange(to_2, 0, 2)
        share = share + exchange(share, 1, 0)
        share, to_3 = lax.optimization_barrier((share, to_3))
        from_3 = exchange(to_3, 0, 3)
        share = share + exchange(share, 3, 0)
        share, to_1 = lax.optimization_barrier((share, to_1))
        from_1 = exchange(to_1, 0, 1)
        flip = 4
        while flip < lax.axis_size("line"):
            share = share + exchange(share, flip + 1, 0)
            flip *= 2
        share, from_2 = lax.optimization_barrier((share, from_2))
        half = share + exchange(share, 1, 1)
        other = exchange(half, 1, 2)
        flows = own_flows(blocks, [from_2, from_3, from_1, own])
        overload, weight, new_mean = last_outputs(
            flows, blocks, half, other, likelihood, draws, proposal_mean
        )
        return (flows, overload, weight, new_mean)

    quarters = head(jnp.arange(QUARTERS, dtype=jnp.int32), *own_buses, n)
    q, groups = lines // QUARTERS, n // LANES
    per_factor = jnp.concatenate(
        [jnp.concatenate([x[j * q : j * q + q] for j in range(groups)], 1) for x in quarters], 0
    )
    base_flow = jnp.concatenate([x[groups * q, :q] for x in quarters])
    block_rows = scenarios // bus_devices
    draws = normals(directions, shifts)
    factors = dot(draws + proposal_mean[None, :], chol_factor, NT, HIGH)
    part = dot(factors, per_factor, NT, HIGH) + base_flow[None, :]
    flows = lax.psum_scatter(part, "bus", scatter_dimension=0, tiled=True)
    rating = line_rating.astype(jnp.float32) * 0.01
    own_normals = lax.dynamic_slice_in_dim(draws, z * block_rows, block_rows, 0)
    likelihood = jnp.exp(-jnp.dot(own_normals, proposal_mean, precision=HIGHEST))
    share = jnp.sum(jax.nn.softplus(SHARP * (jnp.abs(flows) / rating[None, :] - 1.0)), axis=1)
    overload = lax.psum(share, "line") / SHARP / lines_total
    emphasis = likelihood * overload
    moved_part = jnp.dot(emphasis, own_normals, precision=HIGHEST)
    moved, total = lax.psum((moved_part, jnp.sum(emphasis)), "bus")
    return (flows, overload, scenarios * emphasis / total, proposal_mean + moved / total)


def solution(mesh):
    return jax.shard_map(
        per_device,
        mesh=mesh,
        in_specs=(P("line", "bus"), P("bus"), P("bus"), P("bus"), P("line"), P(), P(), P(), P()),
        out_specs=(P("bus", "line"), P("bus"), P("bus"), P()),
        check_vma=False,
    )
```

```python
import math

import jax
import jax.numpy as jnp
from jax import lax
from jax.experimental import pallas as pl
from jax.experimental.pallas import tpu as pltpu
from jax.sharding import PartitionSpec as P

POINTS = 128
SHARP = 8.0
HIGH = lax.Precision.HIGH
HIGHEST = lax.Precision.HIGHEST
NT = (((1,), (1,)), ((), ()))
NN = (((1,), (0,)), ((), ()))
LANES = 128
EXTRA = 16
QUARTERS = 4
MIB = 2**20
CENTRAL = (
    2.81022636e-08, 3.43273939e-07, -3.5233877e-06, -4.39150654e-06, 0.00021858087,
    -0.00125372503, -0.00417768164, 0.246640727, 1.50140941,
)
TAIL = (
    -0.000200214257, 0.000100950558, 0.00134934322, -0.00367342844, 0.00573950773,
    -0.0076224613, 0.00943887047, 1.00167406, 2.83297682,
)


def dot(a, b, dims, precision):
    return lax.dot_general(a, b, dims, precision=precision, preferred_element_type=jnp.float32)


def normal_of(digits):
    x = (2 * (digits >> 7) + 1).astype(jnp.float32) * (2.0 / 16777216.0) - 1.0
    w = -jnp.log((1.0 - x) * (1.0 + x))
    central = w < 5.0
    w = jnp.where(central, w - 2.5, jnp.sqrt(w) - 3.0)
    p = jnp.where(central, CENTRAL[0], TAIL[0])
    for a, b in zip(CENTRAL[1:], TAIL[1:]):
        p = jnp.where(central, a, b) + p * w
    return math.sqrt(2.0) * (p * x)


def block_normals(directions, shifts, start, rows):
    group = min(rows, POINTS)
    n = directions.shape[1]
    digits = jnp.zeros((1, n), jnp.int32)
    bits = group.bit_length() - 1
    lead = min(bits, 3)
    at = lax.broadcasted_iota(jnp.int32, (2**lead, n), 0)
    digits = jnp.zeros((2**lead, n), jnp.int32)
    for b in range(lead):
        digits = digits ^ jnp.where((at >> b & 1) == 1, directions[b : b + 1, :], 0)
    for b in range(lead, bits):
        digits = jnp.concatenate([digits, digits ^ directions[b : b + 1, :]], 0)
    pieces = []
    for j in range(rows // group):
        first = start + j * group
        point = lax.rem(first, POINTS)
        flip = shifts[pl.ds(lax.div(first, POINTS), 1), :]
        for b in range(bits, POINTS.bit_length() - 1):
            flip = flip ^ (directions[b : b + 1, :] * (point >> b & 1))
        pieces.append(normal_of(digits ^ flip))
    return jnp.concatenate(pieces, 0) if len(pieces) > 1 else pieces[0]


def block_plan(buses):
    for first, later in ((3584, 7168), (6272, 6272), (3584, 3584), (1792, 1792), (896, 896), (256, 256)):
        if buses >= first and (buses - first) % later == 0:
            return first, later
    return LANES, LANES


def head(blocks, ptdf, base, gain, factor, n):
    lines, buses = ptdf.shape
    first, later = block_plan(buses)
    steps, rows = 1 + (buses - first) // later, buses // LANES
    q, groups = lines // QUARTERS, n // LANES

    def body(
        blocks_s, p_h, b_h, g_h, f_h, out_0, out_1, out_2, out_3,
        sums, flipped, base_v, p_v, b_v, g_v, f_v, p_sem, v_sem,
    ):
        pairs = ((f_h, f_v), (g_h, g_v), (b_h, b_v))
        small = [pltpu.make_async_copy(h, v, v_sem.at[i]) for i, (h, v) in enumerate(pairs)]
        for copy in small:
            copy.start()

        def place(k):
            return pl.multiple_of(first + (k - 1) * later, LANES)

        def block_copy(k, begin, width):
            at = pl.ds(begin, width)
            return pltpu.make_async_copy(p_h.at[:, at], p_v.at[:, at], p_sem.at[k])

        def start(k, _):
            block_copy(k, place(k), later).start()
            return 0

        block_copy(0, 0, first).start()
        lax.fori_loop(1, steps, start, 0)
        sums[...] = jnp.zeros_like(sums)
        for copy in small:
            copy.wait()

        def add_block(k, begin, width):
            block_copy(k, begin, width).wait()

            def row(v):
                return jnp.concatenate(
                    [v[pl.ds(begin // LANES + j, 1), :] for j in range(width // LANES)], 1
                )

            g = row(g_v)
            p = p_v[:, pl.ds(begin, width)]
            scaled = (p.astype(jnp.float32) * g).astype(jnp.bfloat16)
            own = lax.broadcasted_iota(jnp.int16, (n, width), 0) == row(f_v).astype(jnp.int16)
            hot = jnp.where(own, jnp.bfloat16(1), jnp.bfloat16(0))
            ratio = row(b_v) / g
            high = ratio.astype(jnp.bfloat16)
            low = (ratio - high.astype(jnp.float32)).astype(jnp.bfloat16)
            rest = jnp.zeros((EXTRA - 2, width), jnp.bfloat16)
            left = jnp.concatenate([hot, high, low, rest], 0)
            sums[...] += lax.dot_general(left, scaled, NT, preferred_element_type=jnp.float32)

        def step(k, _):
            add_block(k, place(k), later)
            return 0

        add_block(0, 0, first)
        lax.fori_loop(1, steps, step, 0)
        flipped[...] = sums[:n, :].T
        base_row = sums[n : n + 1, :] + sums[n + 1 : n + 2, :]
        blank = jnp.zeros((1, LANES - q), jnp.float32)
        for d in range(QUARTERS):
            base_v[8 * d : 8 * d + 8, :] = jnp.broadcast_to(
                jnp.concatenate([base_row[:, d * q : d * q + q], blank], 1), (8, LANES)
            )
        for i, out in enumerate((out_0, out_1, out_2, out_3)):
            d = blocks_s[i]
            for j in range(groups):
                out[j * q : j * q + q, :] = flipped[
                    pl.ds(pl.multiple_of(d * q, 8), q), j * LANES : (j + 1) * LANES
                ]
            out[groups * q :, :] = base_v[pl.ds(pl.multiple_of(d * 8, 8), 8), :]

    hbm = pl.BlockSpec(memory_space=pltpu.HBM)
    vmem = pl.BlockSpec(memory_space=pltpu.VMEM)
    return pl.pallas_call(
        body,
        in_specs=[pl.BlockSpec(memory_space=pltpu.SMEM)] + [hbm] * 4,
        out_specs=[vmem] * QUARTERS,
        out_shape=[jax.ShapeDtypeStruct((groups * q + 8, LANES), jnp.float32)] * QUARTERS,
        scratch_shapes=[
            pltpu.VMEM((n + EXTRA, lines), jnp.float32),
            pltpu.VMEM((lines, n), jnp.float32),
            pltpu.VMEM((8 * QUARTERS, LANES), jnp.float32),
            pltpu.VMEM((lines, buses), jnp.bfloat16),
            pltpu.VMEM((rows, LANES), jnp.float32),
            pltpu.VMEM((rows, LANES), jnp.float32),
            pltpu.VMEM((rows, LANES), jnp.int32),
            pltpu.SemaphoreType.DMA((steps,)),
            pltpu.SemaphoreType.DMA((3,)),
        ],
        compiler_params=pltpu.CompilerParams(vmem_limit_bytes=48 * MIB),
        cost_estimate=pl.CostEstimate(
            flops=2 * lines * buses * n, bytes_accessed=2 * lines * buses, transcendentals=0
        ),
        name="segment_sums",
    )(
        blocks,
        *(
            pltpu.with_memory_space_constraint(x, pltpu.HBM)
            for x in (
                ptdf, base.reshape(rows, LANES), gain.reshape(rows, LANES), factor.reshape(rows, LANES),
            )
        ),
    )


def split(x):
    high = x.astype(jnp.bfloat16)
    return high, (x - high.astype(jnp.float32)).astype(jnp.bfloat16)


def all_factors(directions, shifts, chol, mean):
    n = directions.shape[1]
    scenarios = POINTS * shifts.shape[0]
    block = 2 * POINTS

    def body(d_v, s_v, c_v, m_v, f_high, f_low, kept, likelihood, c_high, c_low):
        c_high[...], c_low[...] = split(c_v[...])
        mean_terms = jnp.concatenate([*split(m_v[...]), jnp.zeros((14, n), jnp.bfloat16)], 0)

        def step(k, _):
            at = pl.ds(pl.multiple_of(k * block, block), block)
            draws = block_normals(d_v, s_v, k * block, block)
            kept[at, :] = draws
            high, low = split(draws + m_v[...])
            both = dot(jnp.concatenate([high, low], 0), c_high[...], NT, None)
            factors = both[:block, :] + (both[block:, :] + dot(high, c_low[...], NT, None))
            f_high[at, :], f_low[at, :] = split(factors)
            high, low = split(draws)
            tilt = dot(mean_terms, high, NT, None)
            tilt = tilt[:1, :] + (tilt[1:2, :] + dot(mean_terms, low, NT, None)[:1, :])
            for j in range(block // LANES):
                likelihood[pl.ds(k * (block // LANES) + j, 1), :] = jnp.exp(
                    -tilt[:, j * LANES : (j + 1) * LANES]
                )
            return 0

        lax.fori_loop(0, scenarios // block, step, 0)

    vmem = pl.BlockSpec(memory_space=pltpu.VMEM)
    big = jax.ShapeDtypeStruct((scenarios, n), jnp.bfloat16)
    return pl.pallas_call(
        body,
        in_specs=[vmem] * 4,
        out_specs=[vmem] * 4,
        out_shape=[
            big,
            big,
            jax.ShapeDtypeStruct((scenarios, n), jnp.float32),
            jax.ShapeDtypeStruct((scenarios // LANES, LANES), jnp.float32),
        ],
        scratch_shapes=[pltpu.VMEM((n, n), jnp.bfloat16), pltpu.VMEM((n, n), jnp.bfloat16)],
        compiler_params=pltpu.CompilerParams(vmem_limit_bytes=20 * MIB),
        cost_estimate=pl.CostEstimate(
            flops=6 * scenarios * n * n, bytes_accessed=6 * MIB, transcendentals=2 * scenarios * n
        ),
        name="all_factors",
    )(directions, shifts, chol, mean.reshape(1, n))


def pair_sum(mine, other, later):
    def body(mine_v, other_v, later_v, out, passed):
        out[...] = mine_v[...] + other_v[...]
        passed[...] = later_v[...]

    vmem = pl.BlockSpec(memory_space=pltpu.VMEM)
    return pl.pallas_call(
        body,
        in_specs=[vmem] * 3,
        out_specs=[vmem] * 2,
        out_shape=[jax.ShapeDtypeStruct(mine.shape, jnp.float32)] * 2,
        compiler_params=pltpu.CompilerParams(vmem_limit_bytes=4 * MIB),
        name="pair_sum",
    )(mine, other, later)


def quarter_flows(blocks, mine, beside, far, scale, f_high, f_low, lines_total):
    scenarios, n = f_high.shape
    q = scale.shape[0]
    block, groups = scenarios // QUARTERS, n // LANES

    def body(
        blocks_s, mine_v, beside_v, far_v, scale_v, high_v, low_v, out_0, out_1, out_2, out_3, share, flows
    ):
        total = mine_v[...] + beside_v[...] + far_v[...]
        g = jnp.concatenate([total[j * q : j * q + q, :] for j in range(groups)], 1)
        diagonal = lax.broadcasted_iota(jnp.int32, (q, LANES), 0) == lax.broadcasted_iota(
            jnp.int32, (q, LANES), 1
        )
        base = jnp.sum(
            jnp.where(diagonal, total[groups * q : groups * q + 1, :], 0.0), axis=1, keepdims=True
        )
        g_high, g_low = split(g)
        wide = dot(jnp.concatenate([g_high, g_low], 0), high_v[...], NT, None)
        value = wide[:q, :] + (wide[q:, :] + dot(g_high, low_v[...], NT, None)) + base
        flows[...] = value
        over = jnp.abs(value) * jnp.concatenate([scale_v[...]] * (scenarios // LANES), 1) - SHARP
        soft = jnp.maximum(over, 0.0) + jnp.log(1.0 + jnp.exp(-jnp.abs(over)))
        row = jnp.sum(soft, axis=0, keepdims=True) * (1.0 / SHARP / lines_total)
        share[...] = jnp.concatenate(
            [row[:, j * LANES : (j + 1) * LANES] for j in range(scenarios // LANES)], 0
        )
        for i, out in enumerate((out_0, out_1, out_2, out_3)):
            out[...] = flows[:, pl.ds(pl.multiple_of(blocks_s[i] * block, LANES), block)]

    vmem = pl.BlockSpec(memory_space=pltpu.VMEM)
    shapes = [(q, block)] * QUARTERS + [(scenarios // LANES, LANES)]
    return pl.pallas_call(
        body,
        in_specs=[pl.BlockSpec(memory_space=pltpu.SMEM)] + [vmem] * 6,
        out_specs=[vmem] * 5,
        out_shape=[jax.ShapeDtypeStruct(s, jnp.float32) for s in shapes],
        scratch_shapes=[pltpu.VMEM((q, scenarios), jnp.float32)],
        compiler_params=pltpu.CompilerParams(vmem_limit_bytes=12 * MIB),
        name="quarter_flows",
    )(blocks, mine, beside, far, scale, f_high, f_low)


def own_flows(blocks, parts):
    q, block = parts[0].shape

    def body(blocks_s, part_0, part_1, part_2, part_3, out, whole):
        for i, part in enumerate((part_0, part_1, part_2, part_3)):
            whole[pl.ds(pl.multiple_of(blocks_s[i] * q, 8), q), :] = part[...]
        out[...] = whole[...].T

    vmem = pl.BlockSpec(memory_space=pltpu.VMEM)
    return pl.pallas_call(
        body,
        in_specs=[pl.BlockSpec(memory_space=pltpu.SMEM)] + [vmem] * 4,
        out_specs=vmem,
        out_shape=pltpu.HBM((block, q * QUARTERS), jnp.float32),
        scratch_shapes=[pltpu.VMEM((q * QUARTERS, block), jnp.float32)],
        compiler_params=pltpu.CompilerParams(vmem_limit_bytes=4 * MIB),
        name="own_flows",
    )(blocks, *parts)


def last_outputs(after, blocks, half, other, likelihood, draws, mean):
    scenarios, n = draws.shape
    a, b = scenarios // QUARTERS // LANES, n // LANES

    def body(after_h, blocks_s, half_v, other_v, like_v, draws_v, mean_v, overload, weight, new_mean, kept):
        every = half_v[...] + other_v[...]
        emphasis = like_v[...] * every
        total = jnp.sum(jnp.sum(emphasis, axis=1, keepdims=True), axis=0, keepdims=True)
        columns = emphasis.T
        parts = jnp.zeros((8, n), jnp.float32)
        for g in range(scenarios // LANES):
            piece = draws_v[g * LANES : (g + 1) * LANES, :] * columns[:, g : g + 1]
            parts = parts + jnp.sum(piece.reshape(LANES // 8, 8, n), axis=0)
        moved = jnp.sum(parts, axis=0, keepdims=True)
        moved = jnp.concatenate([moved[:, j * LANES : (j + 1) * LANES] for j in range(b)], 0)
        kept[0] = every
        kept[1] = scenarios * emphasis / total
        at = pl.ds(blocks_s[3] * a, a)
        overload[...] = kept[0, at, :]
        weight[...] = kept[1, at, :]
        new_mean[...] = mean_v[...] + moved / total

    vmem = pl.BlockSpec(memory_space=pltpu.VMEM)
    shapes = [(a, LANES), (a, LANES), (b, LANES)]
    out = pl.pallas_call(
        body,
        in_specs=[pl.BlockSpec(memory_space=pl.ANY), pl.BlockSpec(memory_space=pltpu.SMEM)] + [vmem] * 5,
        out_specs=[vmem] * 3,
        out_shape=[jax.ShapeDtypeStruct(s, jnp.float32) for s in shapes],
        scratch_shapes=[pltpu.VMEM((2, scenarios // LANES, LANES), jnp.float32)],
        compiler_params=pltpu.CompilerParams(vmem_limit_bytes=8 * MIB),
        name="last_outputs",
    )(
        pltpu.with_memory_space_constraint(after, pltpu.HBM), blocks, half, other, likelihood, draws,
        mean.reshape(b, LANES),
    )
    return [x.reshape(-1) for x in out]


def exchange(value, line_flip, bus_flip):
    lines, buses = lax.axis_size("line"), lax.axis_size("bus")
    pairs = [
        (i * buses + j, (i ^ line_flip) * buses + (j ^ bus_flip))
        for i in range(lines)
        for j in range(buses)
    ]
    return lax.ppermute(value, ("line", "bus"), pairs)


def normals(directions, shifts):
    point = jnp.arange(POINTS, dtype=jnp.int32)
    digits = jnp.zeros((POINTS, directions.shape[1]), jnp.int32)
    for b in range(POINTS.bit_length() - 1):
        digits = digits ^ (point >> b & 1)[:, None] * directions[b][None, :]
    return normal_of(digits[None, :, :] ^ shifts[:, None, :]).reshape(-1, directions.shape[1])


def per_device(
    ptdf,
    base_injection,
    injection_gain,
    factor_of_bus,
    line_rating,
    directions,
    shifts,
    chol_factor,
    proposal_mean,
):
    bus_devices = lax.axis_size("bus")
    lines = ptdf.shape[0]
    lines_total = lines * lax.axis_size("line")
    n = directions.shape[1]
    scenarios = POINTS * shifts.shape[0]
    z = lax.axis_index("bus").astype(jnp.int32)
    drawn = (directions, shifts, chol_factor, proposal_mean)
    own_buses = (ptdf, base_injection, injection_gain, factor_of_bus)

    if bus_devices == QUARTERS:
        blocks = jnp.stack([z ^ 2, z ^ 3, z ^ 1, z])
        for_pair, for_far, for_near, mine = head(blocks, *own_buses, n)
        from_near = exchange(for_pair, 0, 1)
        f_high, f_low, draws, likelihood = all_factors(*drawn)
        beside = exchange(for_near, 0, 1)
        far = exchange(for_far + from_near, 0, 3)
        q, block = lines // QUARTERS, scenarios // QUARTERS
        rating = lax.dynamic_slice_in_dim(line_rating, z * q, q).astype(jnp.float32) * 0.01
        scale = jnp.broadcast_to((SHARP / rating)[:, None], (q, LANES))
        to_2, to_3, to_1, own, share = quarter_flows(
            blocks, mine, beside, far, scale, f_high, f_low, lines_total
        )
        from_2 = exchange(to_2, 0, 2)
        share = share + exchange(share, 1, 0)
        share, to_3 = lax.optimization_barrier((share, to_3))
        from_3 = exchange(to_3, 0, 3)
        share = share + exchange(share, 3, 0)
        share, to_1 = lax.optimization_barrier((share, to_1))
        from_1 = exchange(to_1, 0, 1)
        flip = 4
        while flip < lax.axis_size("line"):
            share = share + exchange(share, flip + 1, 0)
            flip *= 2
        share, from_2 = lax.optimization_barrier((share, from_2))
        half = share + exchange(share, 1, 1)
        other = exchange(half, 1, 2)
        flows = own_flows(blocks, [from_2, from_3, from_1, own])
        overload, weight, new_mean = last_outputs(
            flows, blocks, half, other, likelihood, draws, proposal_mean
        )
        return (flows, overload, weight, new_mean)

    quarters = head(jnp.arange(QUARTERS, dtype=jnp.int32), *own_buses, n)
    q, groups = lines // QUARTERS, n // LANES
    per_factor = jnp.concatenate(
        [jnp.concatenate([x[j * q : j * q + q] for j in range(groups)], 1) for x in quarters], 0
    )
    base_flow = jnp.concatenate([x[groups * q, :q] for x in quarters])
    block_rows = scenarios // bus_devices
    draws = normals(directions, shifts)
    factors = dot(draws + proposal_mean[None, :], chol_factor, NT, HIGH)
    part = dot(factors, per_factor, NT, HIGH) + base_flow[None, :]
    flows = lax.psum_scatter(part, "bus", scatter_dimension=0, tiled=True)
    rating = line_rating.astype(jnp.float32) * 0.01
    own_normals = lax.dynamic_slice_in_dim(draws, z * block_rows, block_rows, 0)
    likelihood = jnp.exp(-jnp.dot(own_normals, proposal_mean, precision=HIGHEST))
    share = jnp.sum(jax.nn.softplus(SHARP * (jnp.abs(flows) / rating[None, :] - 1.0)), axis=1)
    overload = lax.psum(share, "line") / SHARP / lines_total
    emphasis = likelihood * overload
    moved_part = jnp.dot(emphasis, own_normals, precision=HIGHEST)
    moved, total = lax.psum((moved_part, jnp.sum(emphasis)), "bus")
    return (flows, overload, scenarios * emphasis / total, proposal_mean + moved / total)


def solution(mesh):
    return jax.shard_map(
        per_device,
        mesh=mesh,
        in_specs=(P("line", "bus"), P("bus"), P("bus"), P("bus"), P("line"), P(), P(), P(), P()),
        out_specs=(P("bus", "line"), P("bus"), P("bus"), P()),
        check_vma=False,
    )
```

```python
import math

import jax
import jax.numpy as jnp
from jax import lax
from jax.experimental import pallas as pl
from jax.experimental.pallas import tpu as pltpu
from jax.sharding import PartitionSpec as P

POINTS = 128
SHARP = 8.0
HIGH = lax.Precision.HIGH
HIGHEST = lax.Precision.HIGHEST
NT = (((1,), (1,)), ((), ()))
NN = (((1,), (0,)), ((), ()))
LANES = 128
EXTRA = 16
QUARTERS = 4
MIB = 2**20
CENTRAL = (
    2.81022636e-08, 3.43273939e-07, -3.5233877e-06, -4.39150654e-06, 0.00021858087,
    -0.00125372503, -0.00417768164, 0.246640727, 1.50140941,
)
TAIL = (
    -0.000200214257, 0.000100950558, 0.00134934322, -0.00367342844, 0.00573950773,
    -0.0076224613, 0.00943887047, 1.00167406, 2.83297682,
)


def dot(a, b, dims, precision):
    return lax.dot_general(a, b, dims, precision=precision, preferred_element_type=jnp.float32)


def normal_of(digits):
    x = (2 * (digits >> 7) + 1).astype(jnp.float32) * (2.0 / 16777216.0) - 1.0
    w = -jnp.log((1.0 - x) * (1.0 + x))
    central = w < 5.0
    w = jnp.where(central, w - 2.5, jnp.sqrt(w) - 3.0)
    p = jnp.where(central, CENTRAL[0], TAIL[0])
    for a, b in zip(CENTRAL[1:], TAIL[1:]):
        p = jnp.where(central, a, b) + p * w
    return math.sqrt(2.0) * (p * x)


def block_normals(directions, shifts, start, rows):
    group = min(rows, POINTS)
    n = directions.shape[1]
    digits = jnp.zeros((1, n), jnp.int32)
    bits = group.bit_length() - 1
    lead = min(bits, 3)
    at = lax.broadcasted_iota(jnp.int32, (2**lead, n), 0)
    digits = jnp.zeros((2**lead, n), jnp.int32)
    for b in range(lead):
        digits = digits ^ jnp.where((at >> b & 1) == 1, directions[b : b + 1, :], 0)
    for b in range(lead, bits):
        digits = jnp.concatenate([digits, digits ^ directions[b : b + 1, :]], 0)
    pieces = []
    for j in range(rows // group):
        first = start + j * group
        point = lax.rem(first, POINTS)
        flip = shifts[pl.ds(lax.div(first, POINTS), 1), :]
        for b in range(bits, POINTS.bit_length() - 1):
            flip = flip ^ (directions[b : b + 1, :] * (point >> b & 1))
        pieces.append(normal_of(digits ^ flip))
    return jnp.concatenate(pieces, 0) if len(pieces) > 1 else pieces[0]


def block_plan(buses):
    for first, later in ((3584, 7168), (6272, 6272), (3584, 3584), (1792, 1792), (896, 896), (256, 256)):
        if buses >= first and (buses - first) % later == 0:
            return first, later
    return LANES, LANES


def head(blocks, ptdf, base, gain, factor, n):
    lines, buses = ptdf.shape
    first, later = block_plan(buses)
    steps, rows = 1 + (buses - first) // later, buses // LANES
    q, groups = lines // QUARTERS, n // LANES

    def body(
        blocks_s, p_h, b_h, g_h, f_h, out_0, out_1, out_2, out_3,
        sums, flipped, base_v, p_v, b_v, g_v, f_v, p_sem, v_sem,
    ):
        pairs = ((f_h, f_v), (g_h, g_v), (b_h, b_v))
        small = [pltpu.make_async_copy(h, v, v_sem.at[i]) for i, (h, v) in enumerate(pairs)]

        def place(k):
            return pl.multiple_of(first + (k - 1) * later, LANES)

        def block_copy(k, begin, width):
            at = pl.ds(begin, width)
            return pltpu.make_async_copy(p_h.at[:, at], p_v.at[:, at], p_sem.at[k])

        def start(k, _):
            block_copy(k, place(k), later).start()
            return 0

        block_copy(0, 0, first).start()
        for copy in small:
            copy.start()
        lax.fori_loop(1, steps, start, 0)
        for copy in small:
            copy.wait()

        def block_sums(k, begin, width):
            block_copy(k, begin, width).wait()

            def row(v):
                return jnp.concatenate(
                    [v[pl.ds(begin // LANES + j, 1), :] for j in range(width // LANES)], 1
                )

            g = row(g_v)
            p = p_v[:, pl.ds(begin, width)]
            scaled = (p.astype(jnp.float32) * g).astype(jnp.bfloat16)
            own = lax.broadcasted_iota(jnp.int16, (n, width), 0) == row(f_v).astype(jnp.int16)
            hot = jnp.where(own, jnp.bfloat16(1), jnp.bfloat16(0))
            ratio = row(b_v) / g
            high = ratio.astype(jnp.bfloat16)
            low = (ratio - high.astype(jnp.float32)).astype(jnp.bfloat16)
            rest = jnp.zeros((EXTRA - 2, width), jnp.bfloat16)
            left = jnp.concatenate([hot, high, low, rest], 0)
            return lax.dot_general(left, scaled, NT, preferred_element_type=jnp.float32)

        def step(k, _):
            sums[...] += block_sums(k, place(k), later)
            return 0

        sums[...] = block_sums(0, 0, first)
        lax.fori_loop(1, steps, step, 0)
        flipped[...] = sums[:n, :].T
        base_row = sums[n : n + 1, :] + sums[n + 1 : n + 2, :]
        blank = jnp.zeros((1, LANES - q), jnp.float32)
        for d in range(QUARTERS):
            base_v[8 * d : 8 * d + 8, :] = jnp.broadcast_to(
                jnp.concatenate([base_row[:, d * q : d * q + q], blank], 1), (8, LANES)
            )
        for i, out in enumerate((out_0, out_1, out_2, out_3)):
            d = blocks_s[i]
            for j in range(groups):
                out[j * q : j * q + q, :] = flipped[
                    pl.ds(pl.multiple_of(d * q, 8), q), j * LANES : (j + 1) * LANES
                ]
            out[groups * q :, :] = base_v[pl.ds(pl.multiple_of(d * 8, 8), 8), :]

    hbm = pl.BlockSpec(memory_space=pltpu.HBM)
    vmem = pl.BlockSpec(memory_space=pltpu.VMEM)
    return pl.pallas_call(
        body,
        in_specs=[pl.BlockSpec(memory_space=pltpu.SMEM)] + [hbm] * 4,
        out_specs=[vmem] * QUARTERS,
        out_shape=[jax.ShapeDtypeStruct((groups * q + 8, LANES), jnp.float32)] * QUARTERS,
        scratch_shapes=[
            pltpu.VMEM((n + EXTRA, lines), jnp.float32),
            pltpu.VMEM((lines, n), jnp.float32),
            pltpu.VMEM((8 * QUARTERS, LANES), jnp.float32),
            pltpu.VMEM((lines, buses), jnp.bfloat16),
            pltpu.VMEM((rows, LANES), jnp.float32),
            pltpu.VMEM((rows, LANES), jnp.float32),
            pltpu.VMEM((rows, LANES), jnp.int32),
            pltpu.SemaphoreType.DMA((steps,)),
            pltpu.SemaphoreType.DMA((3,)),
        ],
        compiler_params=pltpu.CompilerParams(vmem_limit_bytes=48 * MIB),
        cost_estimate=pl.CostEstimate(
            flops=2 * lines * buses * n, bytes_accessed=2 * lines * buses, transcendentals=0
        ),
        name="segment_sums",
    )(
        blocks,
        *(
            pltpu.with_memory_space_constraint(x, pltpu.HBM)
            for x in (
                ptdf, base.reshape(rows, LANES), gain.reshape(rows, LANES), factor.reshape(rows, LANES),
            )
        ),
    )


def split(x):
    high = x.astype(jnp.bfloat16)
    return high, (x - high.astype(jnp.float32)).astype(jnp.bfloat16)


def all_factors(directions, shifts, chol, mean):
    n = directions.shape[1]
    scenarios = POINTS * shifts.shape[0]
    block = 2 * POINTS

    def body(d_v, s_v, c_v, m_v, f_high, f_low, kept, likelihood, c_high, c_low):
        c_high[...], c_low[...] = split(c_v[...])
        mean_terms = jnp.concatenate([*split(m_v[...]), jnp.zeros((14, n), jnp.bfloat16)], 0)

        def step(k, _):
            at = pl.ds(pl.multiple_of(k * block, block), block)
            draws = block_normals(d_v, s_v, k * block, block)
            kept[at, :] = draws
            high, low = split(draws + m_v[...])
            both = dot(jnp.concatenate([high, low], 0), c_high[...], NT, None)
            factors = both[:block, :] + (both[block:, :] + dot(high, c_low[...], NT, None))
            f_high[at, :], f_low[at, :] = split(factors)
            high, low = split(draws)
            tilt = dot(mean_terms, high, NT, None)
            tilt = tilt[:1, :] + (tilt[1:2, :] + dot(mean_terms, low, NT, None)[:1, :])
            for j in range(block // LANES):
                likelihood[pl.ds(k * (block // LANES) + j, 1), :] = jnp.exp(
                    -tilt[:, j * LANES : (j + 1) * LANES]
                )
            return 0

        lax.fori_loop(0, scenarios // block, step, 0)

    vmem = pl.BlockSpec(memory_space=pltpu.VMEM)
    big = jax.ShapeDtypeStruct((scenarios, n), jnp.bfloat16)
    return pl.pallas_call(
        body,
        in_specs=[vmem] * 4,
        out_specs=[vmem] * 4,
        out_shape=[
            big,
            big,
            jax.ShapeDtypeStruct((scenarios, n), jnp.float32),
            jax.ShapeDtypeStruct((scenarios // LANES, LANES), jnp.float32),
        ],
        scratch_shapes=[pltpu.VMEM((n, n), jnp.bfloat16), pltpu.VMEM((n, n), jnp.bfloat16)],
        compiler_params=pltpu.CompilerParams(vmem_limit_bytes=20 * MIB),
        cost_estimate=pl.CostEstimate(
            flops=6 * scenarios * n * n, bytes_accessed=6 * MIB, transcendentals=2 * scenarios * n
        ),
        name="all_factors",
    )(directions, shifts, chol, mean.reshape(1, n))


def pair_sum(mine, other, later):
    def body(mine_v, other_v, later_v, out, passed):
        out[...] = mine_v[...] + other_v[...]
        passed[...] = later_v[...]

    vmem = pl.BlockSpec(memory_space=pltpu.VMEM)
    return pl.pallas_call(
        body,
        in_specs=[vmem] * 3,
        out_specs=[vmem] * 2,
        out_shape=[jax.ShapeDtypeStruct(mine.shape, jnp.float32)] * 2,
        compiler_params=pltpu.CompilerParams(vmem_limit_bytes=4 * MIB),
        name="pair_sum",
    )(mine, other, later)


def quarter_flows(blocks, mine, beside, far, scale, f_high, f_low, lines_total):
    scenarios, n = f_high.shape
    q = scale.shape[0]
    block, groups = scenarios // QUARTERS, n // LANES

    def body(
        blocks_s, mine_v, beside_v, far_v, scale_v, high_v, low_v, out_0, out_1, out_2, out_3, share, flows
    ):
        total = mine_v[...] + beside_v[...] + far_v[...]
        g = jnp.concatenate([total[j * q : j * q + q, :] for j in range(groups)], 1)
        diagonal = lax.broadcasted_iota(jnp.int32, (q, LANES), 0) == lax.broadcasted_iota(
            jnp.int32, (q, LANES), 1
        )
        base = jnp.sum(
            jnp.where(diagonal, total[groups * q : groups * q + 1, :], 0.0), axis=1, keepdims=True
        )
        g_high, g_low = split(g)
        wide = dot(jnp.concatenate([g_high, g_low], 0), high_v[...], NT, None)
        value = wide[:q, :] + (wide[q:, :] + dot(g_high, low_v[...], NT, None)) + base
        flows[...] = value
        over = jnp.abs(value) * jnp.concatenate([scale_v[...]] * (scenarios // LANES), 1) - SHARP
        soft = jnp.maximum(over, 0.0) + jnp.log(1.0 + jnp.exp(-jnp.abs(over)))
        row = jnp.sum(soft, axis=0, keepdims=True) * (1.0 / SHARP / lines_total)
        share[...] = jnp.concatenate(
            [row[:, j * LANES : (j + 1) * LANES] for j in range(scenarios // LANES)], 0
        )
        for i, out in enumerate((out_0, out_1, out_2, out_3)):
            out[...] = flows[:, pl.ds(pl.multiple_of(blocks_s[i] * block, LANES), block)]

    vmem = pl.BlockSpec(memory_space=pltpu.VMEM)
    shapes = [(q, block)] * QUARTERS + [(scenarios // LANES, LANES)]
    return pl.pallas_call(
        body,
        in_specs=[pl.BlockSpec(memory_space=pltpu.SMEM)] + [vmem] * 6,
        out_specs=[vmem] * 5,
        out_shape=[jax.ShapeDtypeStruct(s, jnp.float32) for s in shapes],
        scratch_shapes=[pltpu.VMEM((q, scenarios), jnp.float32)],
        compiler_params=pltpu.CompilerParams(vmem_limit_bytes=12 * MIB),
        name="quarter_flows",
    )(blocks, mine, beside, far, scale, f_high, f_low)


def own_flows(blocks, parts):
    q, block = parts[0].shape

    def body(blocks_s, part_0, part_1, part_2, part_3, out, whole):
        for i, part in enumerate((part_0, part_1, part_2, part_3)):
            whole[pl.ds(pl.multiple_of(blocks_s[i] * q, 8), q), :] = part[...]
        out[...] = whole[...].T

    vmem = pl.BlockSpec(memory_space=pltpu.VMEM)
    return pl.pallas_call(
        body,
        in_specs=[pl.BlockSpec(memory_space=pltpu.SMEM)] + [vmem] * 4,
        out_specs=vmem,
        out_shape=pltpu.HBM((block, q * QUARTERS), jnp.float32),
        scratch_shapes=[pltpu.VMEM((q * QUARTERS, block), jnp.float32)],
        compiler_params=pltpu.CompilerParams(vmem_limit_bytes=4 * MIB),
        name="own_flows",
    )(blocks, *parts)


def last_outputs(after, blocks, half, other, likelihood, draws, mean):
    scenarios, n = draws.shape
    a, b = scenarios // QUARTERS // LANES, n // LANES

    def body(after_h, blocks_s, half_v, other_v, like_v, draws_v, mean_v, overload, weight, new_mean, kept):
        every = half_v[...] + other_v[...]
        emphasis = like_v[...] * every
        total = jnp.sum(jnp.sum(emphasis, axis=1, keepdims=True), axis=0, keepdims=True)
        columns = emphasis.T
        parts = jnp.zeros((8, n), jnp.float32)
        for g in range(scenarios // LANES):
            piece = draws_v[g * LANES : (g + 1) * LANES, :] * columns[:, g : g + 1]
            parts = parts + jnp.sum(piece.reshape(LANES // 8, 8, n), axis=0)
        moved = jnp.sum(parts, axis=0, keepdims=True)
        moved = jnp.concatenate([moved[:, j * LANES : (j + 1) * LANES] for j in range(b)], 0)
        kept[0] = every
        kept[1] = scenarios * emphasis / total
        at = pl.ds(blocks_s[3] * a, a)
        overload[...] = kept[0, at, :]
        weight[...] = kept[1, at, :]
        new_mean[...] = mean_v[...] + moved / total

    vmem = pl.BlockSpec(memory_space=pltpu.VMEM)
    shapes = [(a, LANES), (a, LANES), (b, LANES)]
    out = pl.pallas_call(
        body,
        in_specs=[pl.BlockSpec(memory_space=pl.ANY), pl.BlockSpec(memory_space=pltpu.SMEM)] + [vmem] * 5,
        out_specs=[vmem] * 3,
        out_shape=[jax.ShapeDtypeStruct(s, jnp.float32) for s in shapes],
        scratch_shapes=[pltpu.VMEM((2, scenarios // LANES, LANES), jnp.float32)],
        compiler_params=pltpu.CompilerParams(vmem_limit_bytes=8 * MIB),
        name="last_outputs",
    )(
        pltpu.with_memory_space_constraint(after, pltpu.HBM), blocks, half, other, likelihood, draws,
        mean.reshape(b, LANES),
    )
    return [x.reshape(-1) for x in out]


def exchange(value, line_flip, bus_flip):
    lines, buses = lax.axis_size("line"), lax.axis_size("bus")
    pairs = [
        (i * buses + j, (i ^ line_flip) * buses + (j ^ bus_flip))
        for i in range(lines)
        for j in range(buses)
    ]
    return lax.ppermute(value, ("line", "bus"), pairs)


def normals(directions, shifts):
    point = jnp.arange(POINTS, dtype=jnp.int32)
    digits = jnp.zeros((POINTS, directions.shape[1]), jnp.int32)
    for b in range(POINTS.bit_length() - 1):
        digits = digits ^ (point >> b & 1)[:, None] * directions[b][None, :]
    return normal_of(digits[None, :, :] ^ shifts[:, None, :]).reshape(-1, directions.shape[1])


def per_device(
    ptdf,
    base_injection,
    injection_gain,
    factor_of_bus,
    line_rating,
    directions,
    shifts,
    chol_factor,
    proposal_mean,
):
    bus_devices = lax.axis_size("bus")
    lines = ptdf.shape[0]
    lines_total = lines * lax.axis_size("line")
    n = directions.shape[1]
    scenarios = POINTS * shifts.shape[0]
    z = lax.axis_index("bus").astype(jnp.int32)
    drawn = (directions, shifts, chol_factor, proposal_mean)
    own_buses = (ptdf, base_injection, injection_gain, factor_of_bus)

    if bus_devices == QUARTERS:
        blocks = jnp.stack([z ^ 2, z ^ 3, z ^ 1, z])
        for_pair, for_far, for_near, mine = head(blocks, *own_buses, n)
        from_near = exchange(for_pair, 0, 1)
        f_high, f_low, draws, likelihood = all_factors(*drawn)
        beside = exchange(for_near, 0, 1)
        far = exchange(for_far + from_near, 0, 3)
        q, block = lines // QUARTERS, scenarios // QUARTERS
        rating = lax.dynamic_slice_in_dim(line_rating, z * q, q).astype(jnp.float32) * 0.01
        scale = jnp.broadcast_to((SHARP / rating)[:, None], (q, LANES))
        to_2, to_3, to_1, own, share = quarter_flows(
            blocks, mine, beside, far, scale, f_high, f_low, lines_total
        )
        from_2 = exchange(to_2, 0, 2)
        share = share + exchange(share, 1, 0)
        share, to_3 = lax.optimization_barrier((share, to_3))
        from_3 = exchange(to_3, 0, 3)
        share = share + exchange(share, 3, 0)
        share, to_1 = lax.optimization_barrier((share, to_1))
        from_1 = exchange(to_1, 0, 1)
        flip = 4
        while flip < lax.axis_size("line"):
            share = share + exchange(share, flip + 1, 0)
            flip *= 2
        share, from_2 = lax.optimization_barrier((share, from_2))
        half = share + exchange(share, 1, 1)
        other = exchange(half, 1, 2)
        flows = own_flows(blocks, [from_2, from_3, from_1, own])
        overload, weight, new_mean = last_outputs(
            flows, blocks, half, other, likelihood, draws, proposal_mean
        )
        return (flows, overload, weight, new_mean)

    quarters = head(jnp.arange(QUARTERS, dtype=jnp.int32), *own_buses, n)
    q, groups = lines // QUARTERS, n // LANES
    per_factor = jnp.concatenate(
        [jnp.concatenate([x[j * q : j * q + q] for j in range(groups)], 1) for x in quarters], 0
    )
    base_flow = jnp.concatenate([x[groups * q, :q] for x in quarters])
    block_rows = scenarios // bus_devices
    draws = normals(directions, shifts)
    factors = dot(draws + proposal_mean[None, :], chol_factor, NT, HIGH)
    part = dot(factors, per_factor, NT, HIGH) + base_flow[None, :]
    flows = lax.psum_scatter(part, "bus", scatter_dimension=0, tiled=True)
    rating = line_rating.astype(jnp.float32) * 0.01
    own_normals = lax.dynamic_slice_in_dim(draws, z * block_rows, block_rows, 0)
    likelihood = jnp.exp(-jnp.dot(own_normals, proposal_mean, precision=HIGHEST))
    share = jnp.sum(jax.nn.softplus(SHARP * (jnp.abs(flows) / rating[None, :] - 1.0)), axis=1)
    overload = lax.psum(share, "line") / SHARP / lines_total
    emphasis = likelihood * overload
    moved_part = jnp.dot(emphasis, own_normals, precision=HIGHEST)
    moved, total = lax.psum((moved_part, jnp.sum(emphasis)), "bus")
    return (flows, overload, scenarios * emphasis / total, proposal_mean + moved / total)


def solution(mesh):
    return jax.shard_map(
        per_device,
        mesh=mesh,
        in_specs=(P("line", "bus"), P("bus"), P("bus"), P("bus"), P("line"), P(), P(), P(), P()),
        out_specs=(P("bus", "line"), P("bus"), P("bus"), P()),
        check_vma=False,
    )
```
